128 devices in a mesh: row: 16 (over y_hi, z, core), col: 8 (over x, y_lo).
Axes of the slice: x: 4, y: 4 (y_hi: 2, y_lo: 2; y = y_hi * 2 + y_lo), z: 4, core: 2. Of those that a mesh axis runs over, the one named last changes fastest.
Arguments:
- inverse_factor: float32 [128, 1024, 1024], P(('row', 'col')), as said below
- coupling: float32 [128, 1024, 768], P(('row', 'col'))
- boundary_stiffness: float32 [128, 768, 768], P(('row', 'col')), as said below
- interior_mass: float32 [128, 1024], P(('row', 'col')), may hold values from 0.5 to 2
- boundary_mass: float32 [128, 768], P(('row', 'col')), may hold values from 0.5 to 1
- interface_ids: int32 [128, 768], replicated, may hold values from 0 to 8191, as said below
- trial_modes: float32 [8192, 512], P('col'), may hold values from -4 to 4
Outputs:
- reduced_matrix: float32 [8192, 8192], P('row', 'col')
- reduced_columns: float32 [512, 8192], P('col', 'row')
The draws below stay inside these ranges and needn't reach their ends.
Inputs may be any that keep to these rules, and one draw needn't show every extreme that they name: `interface_ids`: row s lists the 768 interface unknowns of substructure s as six distinct runs of 128 consecutive ids, each starting at a multiple of 128, runs in any order. With g = id // 128 the run's number, three runs of every list have g in one residue class modulo 4, the same class for all lists, and the other three are spread evenly over the other classes; every run number is listed by some substructure. `inverse_factor`: lower triangular with a positive diagonal. Symmetric, and boundary_stiffness[s] - W_s^T W_s is positive definite.
All inputs are finite; a program needn't handle non-finite values.
Results may differ from the reference program's by a relative error of at most 0.0001.
Values sent between devices are 32-bit elements; how exact they have to be, the bound alone decides.
A program may use at most 128 MiB of HBM per device.

```python
import math
import jax
import jax.numpy as jnp
from jax import lax

NI = 1024
IDB = 128
SUB = 32
NB = 768
NG = 8192
MODES = 512
PANEL = 512
SUBS = 128
N_ROW = 16
N_COL = 8


def substructure(key, index):
    sub_key = jax.random.fold_in(jax.random.fold_in(key, 77), index)
    keys = jax.random.split(sub_key, 6)
    diag_part = jnp.exp(jax.random.uniform(keys[0], (NI,), jnp.float32, jnp.log(0.5), jnp.log(1.5)))
    strict = jnp.tril(jax.random.normal(keys[1], (NI, NI), jnp.float32), -1) * (0.5 / NI ** 0.5)
    factor = jnp.diag(diag_part) + strict
    link = jax.random.normal(keys[2], (NI, NB), jnp.float32) * 0.01
    weighted = jnp.dot(factor, link, precision=lax.Precision.HIGHEST)
    random_base = jax.random.normal(keys[4], (NB, NB), jnp.float32)
    dominant = jax.random.uniform(keys[5], (NB,), jnp.float32, 0.5, 1.0)
    stiff = jnp.dot(weighted.T, weighted, precision=lax.Precision.HIGHEST) + jnp.diag(dominant)
    stiff = stiff + 0.3 * jnp.dot(random_base, random_base.T, precision=lax.Precision.HIGHEST) / NB
    stiff = 0.5 * (stiff + stiff.T)
    return (factor, link, stiff)


def draw_everything(key):
    return lax.map(lambda index: substructure(key, index), jnp.arange(N_ROW * N_COL))


def draw_inverse_factor(key, part):
    return draw_everything(key)[0]


def draw_coupling(key, part):
    return draw_everything(key)[1]


def draw_boundary_stiffness(key, part):
    return draw_everything(key)[2]


def draw_interface_ids(key, part):
    total_subs = N_ROW * N_COL
    classes = N_ROW // 4
    per_class = NG // IDB // classes
    spread = 3 // (classes - 1)
    base_key = jax.random.fold_in(key, 5)
    heavy_class = jax.random.randint(jax.random.fold_in(base_key, 1), (), 0, classes)
    offsets = jax.random.permutation(jax.random.fold_in(base_key, 2), total_subs) % per_class
    groups = [(offsets + shift_count) % per_class * classes + heavy_class for shift_count in range(3)]
    for remaining in range(1, classes):
        other_offsets = jax.random.permutation(jax.random.fold_in(base_key, 10 + remaining), total_subs) % per_class
        class_index = (heavy_class + remaining) % classes
        for shift_count in range(spread):
            groups.append((other_offsets + shift_count) % per_class * classes + class_index)
    blocks = jnp.stack(groups, axis=1).astype(jnp.int32)
    order_keys = jax.random.split(jax.random.fold_in(base_key, 3), total_subs)
    orders = jax.vmap(lambda row_key: jax.random.permutation(row_key, 6))(order_keys)
    blocks = jnp.take_along_axis(blocks, orders, axis=1)
    id_values = blocks[:, :, None] * IDB + jnp.arange(IDB, dtype=jnp.int32)[None, None, :]
    return id_values.reshape(total_subs, NB).astype(jnp.int32)


def level_of(stream_key, shape, cuts, smallest, high):
    def one(position, blocks):
        steps = jax.random.uniform(jax.random.fold_in(jax.random.fold_in(stream_key, 6), position), (blocks,), jnp.float32, smallest / len(cuts), high / len(cuts))
        return jnp.repeat(jnp.exp(steps), shape[position] // blocks).reshape((-1,) + (1,) * (len(shape) - position - 1))

    gain = one(*cuts[0])
    for cut in cuts[1:]:
        gain = gain * one(*cut)
    return gain


def gaussian(key, extent, scale, bound, cuts=(), held_as=jnp.bfloat16):
    gain = level_of(key, extent, cuts, -0.22, 0.18) if cuts else 1.0
    array = jax.random.normal(key, extent, jnp.float32) * scale * gain
    return jnp.minimum(jnp.maximum(array, -bound), bound).astype(held_as)


def setup_inputs(seed: int = 0) -> dict:
    key_list = jax.random.split(jax.random.key(seed), 8)
    return {
        "inverse_factor": draw_inverse_factor(jax.random.fold_in(key_list[7], 71), 0),
        "coupling": draw_coupling(jax.random.fold_in(key_list[7], 71), 0),
        "boundary_stiffness": draw_boundary_stiffness(jax.random.fold_in(key_list[7], 71), 0),
        "interior_mass": jnp.clip(jnp.exp(math.log(2.0) - 1.3862944 * jax.random.uniform(key_list[3], (SUBS, NI), jnp.float32) ** level_of(key_list[3], (SUBS, NI), ((0, 128),), -0.2, 0.2)), 0.5, 2.0),
        "boundary_mass": jnp.clip(jnp.exp(math.log(1.0) - 0.6931472 * jax.random.uniform(key_list[4], (SUBS, NB), jnp.float32) ** level_of(key_list[4], (SUBS, NB), ((0, 128),), -0.2, 0.2)), 0.5, 1.0),
        "interface_ids": draw_interface_ids(jax.random.fold_in(key_list[7], 71), 0),
        "trial_modes": gaussian(key_list[6], (NG, MODES), 0.3, 4.0, ((0, 8),), jnp.float32),
    }


highest = lax.Precision.HIGHEST
shift_value = 0.05

def lower_solve(lower, rhs):
    return lax.linalg.triangular_solve(lower, rhs, left_side=True, lower=True)

def condense(factor, link, stiff, inner_mass, outer_mass):
    weighted = jnp.dot(factor, link, precision=highest)
    condensed_k = stiff - jnp.dot(weighted.T, weighted, precision=highest)
    static = jnp.dot(factor.T, weighted, precision=highest)
    condensed_m = jnp.diag(outer_mass) + jnp.dot(static.T, inner_mass[:, None] * static, precision=highest)
    return (condensed_k, condensed_m)

def reference(inverse_factor, coupling, boundary_stiffness, interior_mass, boundary_mass, interface_ids, trial_modes):

    def assemble(carry, items):
        stiff_all, mass_all = carry
        factor, link, stiff, inner_mass, outer_mass, id_values = items
        condensed_k, condensed_m = condense(factor, link, stiff, inner_mass, outer_mass)
        stiff_all = stiff_all.at[id_values[:, None], id_values[None, :]].add(condensed_k)
        mass_all = mass_all.at[id_values[:, None], id_values[None, :]].add(condensed_m)
        return ((stiff_all, mass_all), None)
    zero_matrix = jnp.zeros((NG, NG), jnp.float32)
    (stiff_all, mass_all), _ = lax.scan(assemble, (zero_matrix, zero_matrix), (inverse_factor, coupling, boundary_stiffness, interior_mass, boundary_mass, interface_ids))
    shifted = stiff_all - shift_value * mass_all
    row_blocks = NG // (SUB * N_ROW)
    col_blocks = NG // (SUB * N_COL)
    modes = trial_modes.reshape(N_COL, col_blocks, SUB, MODES).transpose(1, 0, 2, 3).reshape(NG, MODES)
    products = jnp.dot(mass_all, modes, precision=highest)
    lower = jnp.linalg.cholesky(shifted[:PANEL, :PANEL])
    left_solved = lower_solve(lower, shifted[:, :PANEL].T)
    right_solved = lower_solve(lower, shifted[:PANEL, :])
    modes_solved = lower_solve(lower, products[:PANEL, :])
    reduced = shifted - jnp.dot(left_solved.T, right_solved, precision=highest)
    columns = products - jnp.dot(left_solved.T, modes_solved, precision=highest)
    reduced = reduced.reshape(row_blocks, N_ROW, SUB, col_blocks, N_COL, SUB).transpose(1, 0, 2, 4, 3, 5).reshape(NG, NG)
    columns = columns.reshape(row_blocks, N_ROW, SUB, MODES).transpose(3, 1, 0, 2).reshape(MODES, NG)
    return (reduced, columns)
```

```python
import functools

import jax
import jax.numpy as jnp
from jax import lax
from jax.experimental import pallas as pl
from jax.experimental.pallas import tpu as pltpu
from jax.sharding import PartitionSpec as P

SUB = 32
RUN = 128
NG = 8192
PANEL = 512
NI = 1024
NB = 768
ROWS = 16
COLS = 8
SUBS = ROWS * COLS
MODES = 512
SHIFT = 0.05
F32 = jnp.float32
BF16 = jnp.bfloat16
MESH = pl.DeviceIdType.MESH
VMEM_LIMIT = 60 * 1024 * 1024

high = lax.Precision.HIGH
highest = lax.Precision.HIGHEST


def split(x):
    hi = x.astype(BF16)
    return hi, (x - hi.astype(F32)).astype(BF16)


def dot(a, b):
    return jnp.dot(a, b, preferred_element_type=F32)


def dot3(ah, al, bh, bl):
    return dot(ah, bh) + (dot(ah, bl) + dot(al, bh))


def chunk_of_lane(shape):
    return lax.broadcasted_iota(jnp.int32, shape, 1) // SUB


def gather_chunks(tiles, picks, chunk):
    out = None
    for place, (tile, source) in enumerate(picks):
        amount = (place - source) * SUB % RUN
        moved = pltpu.roll(tiles[tile], amount, 1) if amount else tiles[tile]
        out = moved if out is None else jnp.where(chunk == place, moved, out)
    return out


def permute_tiles(tiles):
    chunk = chunk_of_lane(tiles[0].shape)
    out = [gather_chunks(tiles, [(q, u) for q in range(4)], chunk) for u in range(4)]
    for w in range(2):
        out.append(gather_chunks(tiles, [(4 + k % 2, 2 * w + k // 2) for k in range(4)], chunk))
    return out


def pack_half(x, odd):
    low = lax.broadcasted_iota(jnp.int32, (16, RUN), 1) < 64
    top, bottom = x[:16], x[16:]
    if odd:
        return jnp.where(low, pltpu.roll(top, 64, 1), bottom)
    return jnp.where(low, top, pltpu.roll(bottom, 64, 1))


def condense_kernel(
    perm, f_ref, c_ref, b_ref, im_ref, bm_ref,
    oa_ref, ol_ref, chi_ref, clo_ref,
    cph, cpl, fh, fl, fth, ftl, wh, wl, wth, wtl, bp, bmp,
):
    def slot_cols(slot):
        return pl.ds(pl.multiple_of(perm[slot] * RUN, RUN), RUN)

    @pl.loop(0, NI // 32)
    def _(i):
        rows = pl.ds(pl.multiple_of(i * 32, 32), 32)
        out = permute_tiles([c_ref[rows, slot_cols(s)] for s in range(6)])
        for k in range(6):
            hi, lo = split(out[k])
            cph[rows, k * RUN:(k + 1) * RUN] = hi
            cpl[rows, k * RUN:(k + 1) * RUN] = lo

    out = permute_tiles([bm_ref[:, slot_cols(s)] for s in range(6)])
    for k in range(6):
        bmp[:, k * RUN:(k + 1) * RUN] = out[k]

    def permute_rows(slot, u, place):
        rows = pl.ds(pl.multiple_of(perm[slot] * RUN + u * SUB, SUB), SUB)
        target = pl.ds(pl.multiple_of(place, SUB), SUB)
        out = permute_tiles([b_ref[rows, slot_cols(s)] for s in range(6)])
        for k in range(6):
            bp[target, k * RUN:(k + 1) * RUN] = out[k]

    @pl.loop(0, 4)
    def _(u):
        for q in range(4):
            permute_rows(q, u, (u * 4 + q) * SUB)
        for q in range(2):
            permute_rows(4 + q, u, 512 + (u * 2 + q) * SUB)

    root = jnp.sqrt(im_ref[...])
    for i in range(4):
        rows = slice(i * 256, (i + 1) * 256)
        for j in range(i + 1):
            cols = slice(j * 256, (j + 1) * 256)
            block = f_ref[rows, cols]
            fh[rows, cols], fl[rows, cols] = split(block)
            fth[cols, rows], ftl[cols, rows] = split((block * root[:, cols]).T)
    for i in range(4):
        rows = slice(i * 256, (i + 1) * 256)
        depth = (i + 1) * 256
        for n in range(3):
            cols = slice(n * 256, (n + 1) * 256)
            w = dot3(fh[rows, :depth], fl[rows, :depth], cph[:depth, cols], cpl[:depth, cols])
            wh[rows, cols], wl[rows, cols] = split(w)
            wth[cols, rows], wtl[cols, rows] = split(w.T)
    for j in range(3):
        rows = slice(j * 256, (j + 1) * 256)
        for n in range(j, 3):
            cols = slice(n * 256, (n + 1) * 256)
            gram = dot3(wth[rows, :], wtl[rows, :], wh[:, cols], wl[:, cols])
            bp[rows, cols] = bp[rows, cols] - gram
    for i in range(4):
        rows = slice(i * 256, (i + 1) * 256)
        start = i * 256
        for n in range(3):
            cols = slice(n * 256, (n + 1) * 256)
            phi = dot3(fth[rows, start:], ftl[rows, start:], wh[start:, cols], wl[start:, cols])
            cph[rows, cols], cpl[rows, cols] = split(phi)
            wth[cols, rows], wtl[cols, rows] = split(phi.T)

    def put(rows, n, value):
        for half in range(2):
            tile = 2 * n + half
            part = value[:, half * RUN:(half + 1) * RUN]
            if tile < 4:
                oa_ref[tile, rows, :] = part
            else:
                for k in range(8):
                    start = (rows.start + k * SUB) // 2
                    for odd in range(2):
                        ol_ref[2 * (tile - 4) + odd, start:start + 16, :] = pack_half(
                            part[k * SUB:(k + 1) * SUB], odd
                        )

    for j in range(3):
        rows = slice(j * 256, (j + 1) * 256)
        for n in range(j, 3):
            cols = slice(n * 256, (n + 1) * 256)
            mass = dot3(wth[rows, :], wtl[rows, :], cph[:, cols], cpl[:, cols])
            if n == j:
                here = lax.broadcasted_iota(jnp.int32, (256, 256), 0)
                there = lax.broadcasted_iota(jnp.int32, (256, 256), 1)
                mass = mass + jnp.where(here == there, bmp[:, cols], 0.0)
            value = bp[rows, cols] - SHIFT * mass
            chi_ref[rows, cols], clo_ref[rows, cols] = split(mass)
            put(rows, n, value)
            if n != j:
                chi_ref[cols, rows], clo_ref[cols, rows] = split(mass.T)
                put(cols, j, value.T)


def condense(perm, factor, link, stiff, inner, outer):
    vmem = pl.BlockSpec(memory_space=pltpu.VMEM)
    shape = jax.ShapeDtypeStruct
    return pl.pallas_call(
        condense_kernel,
        out_shape=(
            shape((4, NB, RUN), F32),
            shape((4, NB // 2, RUN), F32),
            shape((NB, NB), BF16),
            shape((NB, NB), BF16),
        ),
        in_specs=[pl.BlockSpec(memory_space=pltpu.SMEM)] + [vmem] * 5,
        out_specs=(vmem,) * 4,
        scratch_shapes=[
            pltpu.VMEM((NI, NB), BF16), pltpu.VMEM((NI, NB), BF16),
            pltpu.VMEM((NI, NI), BF16), pltpu.VMEM((NI, NI), BF16),
            pltpu.VMEM((NI, NI), BF16), pltpu.VMEM((NI, NI), BF16),
            pltpu.VMEM((NI, NB), BF16), pltpu.VMEM((NI, NB), BF16),
            pltpu.VMEM((NB, NI), BF16), pltpu.VMEM((NB, NI), BF16),
            pltpu.VMEM((NB, NB), F32), pltpu.VMEM((1, NB), F32),
        ],
        compiler_params=pltpu.CompilerParams(vmem_limit_bytes=VMEM_LIMIT),
        cost_estimate=pl.CostEstimate(flops=11 * 10**9, bytes_accessed=16 * 10**6, transcendentals=0),
        name="condense",
    )(perm, factor, link, stiff, inner, outer)


def modes_pack_kernel(runs, meta, q_ref, out_ref, sem):
    light = meta[2]
    copies = []
    for c in range(COLS):
        for q in range(4):
            slot = jnp.where(light == 1, 4 + min(q, 1), q)
            block = runs[(meta[0] * COLS + c) * 6 + slot] // 2
            copies.append(
                pltpu.make_async_copy(
                    q_ref.at[pl.ds(pl.multiple_of(block * SUB, SUB), SUB)],
                    out_ref.at[c, pl.ds(q * SUB, SUB)],
                    sem.at[c * 4 + q],
                )
            )
    for copy in copies:
        copy.start()
    for copy in copies:
        copy.wait()


def modes_pack(runs, meta, modes):
    smem = pl.BlockSpec(memory_space=pltpu.SMEM)
    anywhere = pl.BlockSpec(memory_space=pl.ANY)
    return pl.pallas_call(
        modes_pack_kernel,
        out_shape=jax.ShapeDtypeStruct((COLS, RUN, MODES), F32),
        in_specs=[smem, smem, anywhere],
        out_specs=anywhere,
        scratch_shapes=[pltpu.SemaphoreType.DMA((32,))],
        name="modes_pack",
    )(runs, meta, modes)


def products_kernel(meta, chi_ref, clo_ref, q_ref, out_ref, qh, ql):
    parity = meta[3]
    for u in range(4):
        block = q_ref[parity * 4 + u]
        rows = slice(u * RUN, (u + 1) * RUN)
        qh[rows, :], ql[rows, :] = split(block)
        block = q_ref[(1 - parity) * 4 + u, :64, :]
        rows = slice(512 + u * 64, 512 + (u + 1) * 64)
        qh[rows, :], ql[rows, :] = split(block)
    for j in range(3):
        rows = slice(j * 256, (j + 1) * 256)
        for n in range(2):
            cols = slice(n * 256, (n + 1) * 256)
            z = dot3(chi_ref[rows, :], clo_ref[rows, :], qh[:, cols], ql[:, cols])
            for half in range(2):
                for k in range(8):
                    start = (j * 256 + k * SUB) // 2
                    part = z[k * SUB:(k + 1) * SUB, half * RUN:(half + 1) * RUN]
                    for odd in range(2):
                        out_ref[n * 4 + half * 2 + odd, start:start + 16, :] = pack_half(part, odd)


def products(meta, chi, clo, modes):
    vmem = pl.BlockSpec(memory_space=pltpu.VMEM)
    return pl.pallas_call(
        products_kernel,
        out_shape=jax.ShapeDtypeStruct((COLS, NB // 2, RUN), F32),
        in_specs=[pl.BlockSpec(memory_space=pltpu.SMEM)] + [vmem] * 3,
        out_specs=vmem,
        scratch_shapes=[pltpu.VMEM((NB, MODES), BF16)] * 2,
        compiler_params=pltpu.CompilerParams(vmem_limit_bytes=VMEM_LIMIT),
        cost_estimate=pl.CostEstimate(flops=18 * 10**8, bytes_accessed=6 * 10**6, transcendentals=0),
        name="products",
    )(meta, chi, clo, modes)


def exchange_kernel(heavy, oa, ol, oz, in_a, in_z, send_a, recv_a, send_z, recv_z, local_sem):
    row, col = lax.axis_index("row"), lax.axis_index("col")
    me = row * COLS + col
    barrier = pltpu.get_barrier_semaphore()

    @pl.loop(1, SUBS)
    def _(i):
        other = lax.rem(me + i, SUBS)
        pl.semaphore_signal(
            barrier, inc=1, device_id=(other // COLS, lax.rem(other, COLS)), device_id_type=MESH
        )

    pl.semaphore_wait(barrier, SUBS - 1)

    def place(target):
        target_row, target_col = target // COLS, lax.rem(target, COLS)
        rel = lax.rem(target_row // 4 + 4 - heavy, 4)
        light = lax.rem(target_col // 4 + heavy, 2)
        return target_row, target_col, rel, lax.rem(target_row, 4), light, lax.rem(target_col, 4)

    def first_row(rel, t):
        start = jnp.where(rel == 0, t * 128, jnp.where(rel == 2, t * 128 + 96, 512 + t * 64))
        return jnp.where(rel == 3, start + 32, start)

    def parts(target, use):
        target_row, target_col, rel, t, light, u = place(target)
        start = first_row(rel, t)
        for light_row in range(2):
            count = 32 if light_row else 96

            @pl.when((rel != 0) == (light_row == 1))
            def _():
                half = pl.multiple_of(start // 2, 16)
                use(
                    "z",
                    oz.at[target_col, pl.ds(half, count // 2)],
                    count // 2, target_row, target_col,
                )

                @pl.when(light == 0)
                def _():
                    use(
                        "a",
                        oa.at[u, pl.ds(pl.multiple_of(start, 32), count)],
                        count, target_row, target_col,
                    )

                @pl.when(light == 1)
                def _():
                    use(
                        "a",
                        ol.at[u, pl.ds(half, count // 2)],
                        count // 2, target_row, target_col,
                    )

    def box(kind, source, count):
        ref = in_a if kind == "a" else in_z
        return ref.at[pl.ds(pl.multiple_of(source * count, 16), count)]

    def remote(kind, source_ref, count, target_row, target_col):
        send, recv = (send_a, recv_a) if kind == "a" else (send_z, recv_z)
        return pltpu.make_async_remote_copy(
            src_ref=source_ref,
            dst_ref=box(kind, me, count),
            send_sem=send.at[target_row * COLS + target_col],
            recv_sem=recv.at[me],
            device_id=(target_row, target_col),
            device_id_type=MESH,
        )

    def keep(kind, source_ref, count, target_row, target_col):
        copy = pltpu.make_async_copy(source_ref, box(kind, me, count), local_sem)
        copy.start()
        copy.wait()

    @pl.loop(1, SUBS)
    def _(i):
        parts(lax.rem(me + i, SUBS), lambda *a: remote(*a).start())

    parts(me, keep)

    def arrived(kind, source_ref, count, target_row, target_col):
        recv = recv_a if kind == "a" else recv_z

        @pl.loop(1, SUBS)
        def _(i):
            source = lax.rem(me + i, SUBS)
            here = box(kind, source, count)
            pltpu.make_async_copy(here, here, recv.at[source]).wait()

    parts(me, arrived)

    @pl.loop(1, SUBS)
    def _(i):
        parts(lax.rem(me + i, SUBS), lambda *a: remote(*a).wait_send())


def exchange(heavy, oa, ol, oz):
    anywhere = pl.BlockSpec(memory_space=pl.ANY)
    shape = jax.ShapeDtypeStruct
    return pl.pallas_call(
        functools.partial(exchange_kernel, heavy),
        out_shape=(shape((SUBS * 96, RUN), F32), shape((SUBS * 48, RUN), F32)),
        in_specs=[anywhere] * 3,
        out_specs=(anywhere,) * 2,
        scratch_shapes=[pltpu.SemaphoreType.DMA((SUBS,))] * 4 + [pltpu.SemaphoreType.DMA],
        compiler_params=pltpu.CompilerParams(collective_id=1 + heavy, has_side_effects=True),
        name=f"exchange_{heavy}",
    )(oa, ol, oz)


def place_kernel(runs, meta, in_a, in_z, a_ref, z_ref, acc, zacc, ztall):
    rel, light = meta[1], meta[2]
    acc[...] = jnp.zeros_like(acc)
    zacc[...] = jnp.zeros_like(zacc)

    def run(light_row, light_col):
        slots = [jnp.where(rel == 2, 3, jnp.where(rel == 1, 4, 5))] if light_row else [0, 1, 2]
        col_slots = [4, 5] if light_col else [0, 1, 2, 3]
        number = len(slots)
        height = 16 if light_col else SUB
        chunk = chunk_of_lane((height, RUN))

        @pl.loop(0, SUBS)
        def _(s):
            at = [runs[s * 6 + slot] // 4 for slot in slots]
            to = [runs[s * 6 + slot] // 2 for slot in col_slots]
            for p in range(number):
                zrows = pl.ds(pl.multiple_of(at[p] * 16, 16), 16)
                zacc[zrows, :] += in_z[pl.ds(pl.multiple_of((s * number + p) * 16, 16), 16), :]
            for p in range(number):
                piece = in_a[pl.ds(pl.multiple_of((s * number + p) * height, height), height), :]
                new = []
                for q in range(len(to)):
                    tile, place = to[q] // 4, lax.rem(to[q], 4)
                    for half in range(SUB // height):
                        rows = pl.ds(pl.multiple_of(at[p] * SUB + half * height, height), height)
                        moved = pltpu.roll(piece, lax.rem(place + 8 - q - 2 * half, 4) * SUB, 1)
                        moved = jnp.where(chunk == place, moved, 0.0)
                        new.append((q, tile, rows, acc[q, tile, rows, :] + moved))
                for q, tile, rows, value in new:
                    acc[q, tile, rows, :] = value

    for light_row in range(2):
        for light_col in range(2):
            pl.when(((rel != 0) == (light_row == 1)) & (light == light_col))(
                functools.partial(run, light_row, light_col)
            )
    for k in range(8):
        a_ref[:, k * RUN:(k + 1) * RUN] = (acc[0, k] + acc[1, k]) + (acc[2, k] + acc[3, k])
    for k in range(16):
        piece = zacc[k * 16:(k + 1) * 16, :]
        ztall[k * SUB:k * SUB + 16, :] = piece
        ztall[k * SUB + 16:(k + 1) * SUB, :] = pltpu.roll(piece, 64, 1)
    z_ref[...] = ztall[...].T[:64, :]


def place(runs, meta, in_a, in_z):
    smem = pl.BlockSpec(memory_space=pltpu.SMEM)
    vmem = pl.BlockSpec(memory_space=pltpu.VMEM)
    shape = jax.ShapeDtypeStruct
    return pl.pallas_call(
        place_kernel,
        out_shape=(shape((512, 1024), F32), shape((64, 512), F32)),
        in_specs=[smem, smem, vmem, vmem],
        out_specs=(vmem, vmem),
        scratch_shapes=[
            pltpu.VMEM((4, 8, 512, RUN), F32),
            pltpu.VMEM((256, RUN), F32),
            pltpu.VMEM((512, RUN), F32),
        ],
        compiler_params=pltpu.CompilerParams(vmem_limit_bytes=VMEM_LIMIT),
        name="place",
    )(runs, meta, in_a, in_z)


def lower_solve(lower, rhs):
    return lax.linalg.triangular_solve(lower, rhs, left_side=True, lower=True)


def tmatmul(left, right):
    return lax.dot_general(left, right, (((0,), (0,)), ((), ())), precision=high)


def slot_order(interface_ids):
    runs = interface_ids[:, ::RUN] // RUN
    kinds = runs % 4
    first = kinds[0]
    heavy = jnp.argmax(jnp.sum(first[None, :] == jnp.arange(4)[:, None], axis=1)).astype(jnp.int32)
    rel = (kinds - heavy) % 4
    key = jnp.where(rel == 1, 2, jnp.where(rel == 2, 1, rel)) * 8 + jnp.arange(6)
    slot = jnp.sum(key[:, None, :] < key[:, :, None], axis=2)
    hit = slot[:, :, None] == jnp.arange(6)
    ordered = jnp.sum(jnp.where(hit, runs[:, :, None], 0), axis=1)
    origin = jnp.sum(jnp.where(hit, jnp.arange(6)[None, :, None], 0), axis=1)
    return heavy, ordered.astype(jnp.int32), origin.astype(jnp.int32)


def body(
    inverse_factor,
    coupling,
    boundary_stiffness,
    interior_mass,
    boundary_mass,
    interface_ids,
    trial_modes,
):
    row, col = lax.axis_index("row"), lax.axis_index("col")
    heavy, ordered, origin = slot_order(interface_ids)
    perm = lax.dynamic_index_in_dim(origin, row * COLS + col, 0, keepdims=False)
    runs = ordered.reshape(-1)
    meta = jnp.stack([row, (row // 4 + 4 - heavy) % 4, (col // 4 + heavy) % 2, heavy % 2]).astype(jnp.int32)
    sent = modes_pack(runs, meta, trial_modes)
    modes = lax.all_to_all(sent, "col", split_axis=0, concat_axis=0, tiled=True)
    oa, ol, chi, clo = condense(
        perm, inverse_factor[0], coupling[0], boundary_stiffness[0], interior_mass, boundary_mass
    )
    oz = products(meta, chi, clo, modes)
    in_a, in_z = lax.switch(heavy, [functools.partial(exchange, h) for h in range(4)], oa, ol, oz)
    shifted, modes_local = place(runs, meta, in_a, in_z)

    panel_row_count = PANEL // ROWS
    panel_col_count = PANEL // COLS
    cols_gathered = lax.all_gather(shifted[:, :panel_col_count], "col", axis=1, tiled=True)
    panel_cols = (
        cols_gathered.reshape(-1, COLS, panel_col_count // SUB, SUB)
        .transpose(0, 2, 1, 3)
        .reshape(-1, PANEL)
    )
    panel_rows = lax.all_gather(shifted[:panel_row_count, :], "row", axis=0, tiled=True)
    corner = lax.all_gather(panel_cols[:panel_row_count, :], "row", axis=0, tiled=True)
    lower = jnp.linalg.cholesky(corner)
    left_solved = lower_solve(lower, panel_cols.T)
    right_solved = lower_solve(lower, panel_rows)
    reduced_matrix = shifted - tmatmul(left_solved, right_solved)
    panel_modes = lax.all_gather(modes_local[:, :panel_row_count], "row", axis=1, tiled=True)
    modes_solved = lower_solve(lower, panel_modes.T)
    reduced_columns = modes_local - tmatmul(modes_solved, left_solved)
    return (reduced_matrix, reduced_columns)


def solution(mesh):
    return jax.shard_map(
        body,
        mesh=mesh,
        in_specs=(
            P(("row", "col"), None, None),
            P(("row", "col"), None, None),
            P(("row", "col"), None, None),
            P(("row", "col"), None),
            P(("row", "col"), None),
            P(),
            P("col", None),
        ),
        out_specs=(P("row", "col"), P("col", "row")),
        check_vma=False,
    )
```

```python
import functools

import jax
import jax.numpy as jnp
from jax import lax
from jax.experimental import pallas as pl
from jax.experimental.pallas import tpu as pltpu
from jax.sharding import PartitionSpec as P

SUB = 32
RUN = 128
NG = 8192
PANEL = 512
NI = 1024
NB = 768
ROWS = 16
COLS = 8
SUBS = ROWS * COLS
MODES = 512
SHIFT = 0.05
F32 = jnp.float32
BF16 = jnp.bfloat16
MESH = pl.DeviceIdType.MESH
VMEM_LIMIT = 60 * 1024 * 1024

high = lax.Precision.HIGH
highest = lax.Precision.HIGHEST


def split(x):
    hi = x.astype(BF16)
    return hi, (x - hi.astype(F32)).astype(BF16)


def dot(a, b):
    return jnp.dot(a, b, preferred_element_type=F32)


def dot3(ah, al, bh, bl):
    return dot(ah, bh) + (dot(ah, bl) + dot(al, bh))


def chunk_of_lane(shape):
    return lax.broadcasted_iota(jnp.int32, shape, 1) // SUB


def gather_chunks(tiles, picks, chunk):
    out = None
    for place, (tile, source) in enumerate(picks):
        amount = (place - source) * SUB % RUN
        moved = pltpu.roll(tiles[tile], amount, 1) if amount else tiles[tile]
        out = moved if out is None else jnp.where(chunk == place, moved, out)
    return out


def permute_tiles(tiles):
    chunk = chunk_of_lane(tiles[0].shape)
    out = [gather_chunks(tiles, [(q, u) for q in range(4)], chunk) for u in range(4)]
    for w in range(2):
        out.append(gather_chunks(tiles, [(4 + k % 2, 2 * w + k // 2) for k in range(4)], chunk))
    return out


def pack_half(x, odd):
    low = lax.broadcasted_iota(jnp.int32, (16, RUN), 1) < 64
    top, bottom = x[:16], x[16:]
    if odd:
        return jnp.where(low, pltpu.roll(top, 64, 1), bottom)
    return jnp.where(low, top, pltpu.roll(bottom, 64, 1))


def condense_kernel(
    perm, f_ref, c_ref, b_ref, im_ref, bm_ref,
    oa_ref, ol_ref, chi_ref, clo_ref, corner_ref,
    cph, cpl, fh, fl, fth, ftl, wh, wl, wth, wtl, bp, bmp,
):
    def slot_cols(slot):
        return pl.ds(pl.multiple_of(perm[slot] * RUN, RUN), RUN)

    @pl.loop(0, NI // 32)
    def _(i):
        rows = pl.ds(pl.multiple_of(i * 32, 32), 32)
        out = permute_tiles([c_ref[rows, slot_cols(s)] for s in range(6)])
        for k in range(6):
            hi, lo = split(out[k])
            cph[rows, k * RUN:(k + 1) * RUN] = hi
            cpl[rows, k * RUN:(k + 1) * RUN] = lo

    out = permute_tiles([bm_ref[:, slot_cols(s)] for s in range(6)])
    for k in range(6):
        bmp[:, k * RUN:(k + 1) * RUN] = out[k]

    def permute_rows(slot, u, place):
        rows = pl.ds(pl.multiple_of(perm[slot] * RUN + u * SUB, SUB), SUB)
        target = pl.ds(pl.multiple_of(place, SUB), SUB)
        out = permute_tiles([b_ref[rows, slot_cols(s)] for s in range(6)])
        for k in range(6):
            bp[target, k * RUN:(k + 1) * RUN] = out[k]

    @pl.loop(0, 4)
    def _(u):
        for q in range(4):
            permute_rows(q, u, (u * 4 + q) * SUB)
        for q in range(2):
            permute_rows(4 + q, u, 512 + (u * 2 + q) * SUB)

    root = jnp.sqrt(im_ref[...])
    for i in range(4):
        rows = slice(i * 256, (i + 1) * 256)
        for j in range(i + 1):
            cols = slice(j * 256, (j + 1) * 256)
            block = f_ref[rows, cols]
            fh[rows, cols], fl[rows, cols] = split(block)
            fth[cols, rows], ftl[cols, rows] = split((block * root[:, cols]).T)
    for i in range(4):
        rows = slice(i * 256, (i + 1) * 256)
        depth = (i + 1) * 256
        for n in range(3):
            cols = slice(n * 256, (n + 1) * 256)
            w = dot3(fh[rows, :depth], fl[rows, :depth], cph[:depth, cols], cpl[:depth, cols])
            wh[rows, cols], wl[rows, cols] = split(w)
            wth[cols, rows], wtl[cols, rows] = split(w.T)
    for j in range(3):
        rows = slice(j * 256, (j + 1) * 256)
        for n in range(j, 3):
            cols = slice(n * 256, (n + 1) * 256)
            gram = dot3(wth[rows, :], wtl[rows, :], wh[:, cols], wl[:, cols])
            bp[rows, cols] = bp[rows, cols] - gram
    for i in range(4):
        rows = slice(i * 256, (i + 1) * 256)
        start = i * 256
        for n in range(3):
            cols = slice(n * 256, (n + 1) * 256)
            phi = dot3(fth[rows, start:], ftl[rows, start:], wh[start:, cols], wl[start:, cols])
            cph[rows, cols], cpl[rows, cols] = split(phi)
            wth[cols, rows], wtl[cols, rows] = split(phi.T)

    def put(rows, n, value):
        bp[rows, n * 256:(n + 1) * 256] = value
        for half in range(2):
            tile = 2 * n + half
            part = value[:, half * RUN:(half + 1) * RUN]
            if tile < 4:
                oa_ref[tile, rows, :] = part
            else:
                for k in range(8):
                    start = (rows.start + k * SUB) // 2
                    for odd in range(2):
                        ol_ref[2 * (tile - 4) + odd, start:start + 16, :] = pack_half(
                            part[k * SUB:(k + 1) * SUB], odd
                        )

    for j in range(3):
        rows = slice(j * 256, (j + 1) * 256)
        for n in range(j, 3):
            cols = slice(n * 256, (n + 1) * 256)
            mass = dot3(wth[rows, :], wtl[rows, :], cph[:, cols], cpl[:, cols])
            if n == j:
                here = lax.broadcasted_iota(jnp.int32, (256, 256), 0)
                there = lax.broadcasted_iota(jnp.int32, (256, 256), 1)
                mass = mass + jnp.where(here == there, bmp[:, cols], 0.0)
            value = bp[rows, cols] - SHIFT * mass
            chi_ref[rows, cols], clo_ref[rows, cols] = split(mass)
            put(rows, n, value)
            if n != j:
                chi_ref[cols, rows], clo_ref[cols, rows] = split(mass.T)
                put(cols, j, value.T)

    corner_ref[...] = jnp.zeros_like(corner_ref)
    low = lax.broadcasted_iota(jnp.int32, (16, RUN), 1)
    for gi in range(4):
        for gj in range(4):
            pi, pj = perm[6 + gi], perm[6 + gj]

            @pl.when((pi >= 0) & (pj >= 0))
            def _():
                @pl.loop(0, 16)
                def _(k):
                    t, u = k // 4, lax.rem(k, 4)
                    row = jnp.where(pi < 4, t * RUN + pi * SUB, 512 + t * 64 + (pi - 4) * SUB)
                    tile = jnp.where(pj < 4, u, 4 + u // 2)
                    place = jnp.where(pj < 4, pj, lax.rem(u, 2) * 2 + pj - 4)
                    x = bp[pl.ds(pl.multiple_of(row, SUB), SUB), pl.ds(pl.multiple_of(tile * RUN, RUN), RUN)]
                    start = ((gi * 4 + t) * COLS + (gj % 2) * 4 + u) * 16
                    where = pl.ds(pl.multiple_of(start, 16), 16)
                    base = (gj // 2) * SUB
                    top = pltpu.roll(x[:16], lax.rem(base // SUB + 4 - place, 4) * SUB, 1)
                    bottom = pltpu.roll(x[16:], lax.rem(base // SUB + 6 - place, 4) * SUB, 1)
                    old = corner_ref[where, :]
                    old = jnp.where((low >= base) & (low < base + SUB), top, old)
                    corner_ref[where, :] = jnp.where((low >= base + 64) & (low < base + 96), bottom, old)


def condense(perm, factor, link, stiff, inner, outer):
    vmem = pl.BlockSpec(memory_space=pltpu.VMEM)
    shape = jax.ShapeDtypeStruct
    return pl.pallas_call(
        condense_kernel,
        out_shape=(
            shape((4, NB, RUN), F32),
            shape((4, NB // 2, RUN), F32),
            shape((NB, NB), BF16),
            shape((NB, NB), BF16),
            shape((SUBS * 16, RUN), F32),
        ),
        in_specs=[pl.BlockSpec(memory_space=pltpu.SMEM)] + [vmem] * 5,
        out_specs=(vmem,) * 5,
        scratch_shapes=[
            pltpu.VMEM((NI, NB), BF16), pltpu.VMEM((NI, NB), BF16),
            pltpu.VMEM((NI, NI), BF16), pltpu.VMEM((NI, NI), BF16),
            pltpu.VMEM((NI, NI), BF16), pltpu.VMEM((NI, NI), BF16),
            pltpu.VMEM((NI, NB), BF16), pltpu.VMEM((NI, NB), BF16),
            pltpu.VMEM((NB, NI), BF16), pltpu.VMEM((NB, NI), BF16),
            pltpu.VMEM((NB, NB), F32), pltpu.VMEM((1, NB), F32),
        ],
        compiler_params=pltpu.CompilerParams(vmem_limit_bytes=VMEM_LIMIT),
        cost_estimate=pl.CostEstimate(flops=11 * 10**9, bytes_accessed=16 * 10**6, transcendentals=0),
        name="condense",
    )(perm, factor, link, stiff, inner, outer)


def modes_pack_kernel(runs, meta, q_ref, out_ref):
    light = meta[2]
    for c in range(COLS):
        for q in range(4):
            slot = jnp.where(light == 1, 4 + min(q, 1), q)
            block = runs[(meta[0] * COLS + c) * 6 + slot] // 2
            out_ref[c, q * SUB:(q + 1) * SUB, :] = q_ref[pl.ds(pl.multiple_of(block * SUB, SUB), SUB), :]


def modes_pack(runs, meta, modes):
    smem = pl.BlockSpec(memory_space=pltpu.SMEM)
    vmem = pl.BlockSpec(memory_space=pltpu.VMEM)
    return pl.pallas_call(
        modes_pack_kernel,
        out_shape=jax.ShapeDtypeStruct((COLS, RUN, MODES), F32),
        in_specs=[smem, smem, vmem],
        out_specs=vmem,
        compiler_params=pltpu.CompilerParams(vmem_limit_bytes=VMEM_LIMIT),
        name="modes_pack",
    )(runs, meta, modes)


def products_kernel(meta, chi_ref, clo_ref, q_ref, out_ref, qh, ql):
    parity = meta[3]
    for u in range(4):
        block = q_ref[parity * 4 + u]
        rows = slice(u * RUN, (u + 1) * RUN)
        qh[rows, :], ql[rows, :] = split(block)
        block = q_ref[(1 - parity) * 4 + u, :64, :]
        rows = slice(512 + u * 64, 512 + (u + 1) * 64)
        qh[rows, :], ql[rows, :] = split(block)
    for j in range(3):
        rows = slice(j * 256, (j + 1) * 256)
        for n in range(2):
            cols = slice(n * 256, (n + 1) * 256)
            z = dot3(chi_ref[rows, :], clo_ref[rows, :], qh[:, cols], ql[:, cols])
            for half in range(2):
                for k in range(8):
                    start = (j * 256 + k * SUB) // 2
                    part = z[k * SUB:(k + 1) * SUB, half * RUN:(half + 1) * RUN]
                    for odd in range(2):
                        out_ref[n * 4 + half * 2 + odd, start:start + 16, :] = pack_half(part, odd)


def products(meta, chi, clo, modes):
    vmem = pl.BlockSpec(memory_space=pltpu.VMEM)
    return pl.pallas_call(
        products_kernel,
        out_shape=jax.ShapeDtypeStruct((COLS, NB // 2, RUN), F32),
        in_specs=[pl.BlockSpec(memory_space=pltpu.SMEM)] + [vmem] * 3,
        out_specs=vmem,
        scratch_shapes=[pltpu.VMEM((NB, MODES), BF16)] * 2,
        compiler_params=pltpu.CompilerParams(vmem_limit_bytes=VMEM_LIMIT),
        cost_estimate=pl.CostEstimate(flops=18 * 10**8, bytes_accessed=6 * 10**6, transcendentals=0),
        name="products",
    )(meta, chi, clo, modes)


def eye(n):
    return jnp.where(
        lax.broadcasted_iota(jnp.int32, (n, n), 0) == lax.broadcasted_iota(jnp.int32, (n, n), 1), 1.0, 0.0
    )


def exact(a, b, axis=1):
    return lax.dot_general(
        a, b, (((axis,), (0,)), ((), ())), precision=highest, preferred_element_type=F32
    )


def invert_factor(m_ref, inv_ref, work):
    inv_ref[...] = jnp.zeros_like(inv_ref)
    lane = lax.broadcasted_iota(jnp.int32, (1, RUN), 1)
    height = lax.broadcasted_iota(jnp.int32, (RUN, 1), 0)
    for k in range(4):
        block = slice(k * RUN, (k + 1) * RUN)
        work[:, :RUN] = m_ref[block, block]
        work[:, RUN:] = eye(RUN)

        @pl.loop(0, RUN)
        def _(j):
            row = work[pl.ds(j, 1), :]
            here = lane == j
            pivot = jnp.sum(jnp.where(here, row[:, :RUN], 0.0), axis=1, keepdims=True)
            column = jnp.sum(jnp.where(here, work[:, :RUN], 0.0), axis=1, keepdims=True)
            scale = jnp.where(height > j, column / pivot, 0.0)
            work[...] = work[...] - scale * row
            work[pl.ds(j, 1), :] = row * lax.rsqrt(pivot)

        t = work[:, RUN:]
        left = None
        if k:
            left = exact(t, inv_ref[block, :k * RUN])
            inv_ref[block, :k * RUN] = left
        inv_ref[block, block] = t
        if k < 3:
            x = exact(t, m_ref[block, (k + 1) * RUN:])
            below = slice((k + 1) * RUN, 512)
            m_ref[below, below] = m_ref[below, below] - exact(x, x, 0)
            if k:
                inv_ref[below, :k * RUN] = inv_ref[below, :k * RUN] - exact(x, left, 0)
            inv_ref[below, block] = inv_ref[below, block] - exact(x, t, 0)


def exchange_kernel(
    heavy, corner, oa, ol, oz, in_a, in_z, inv_ref,
    send_a, recv_a, send_z, recv_z, send_c, recv_c, send_g, recv_g, local_sem,
    parts_box, whole_box, m_ref, work,
):
    row, col = lax.axis_index("row"), lax.axis_index("col")
    me = row * COLS + col
    barrier = pltpu.get_barrier_semaphore()

    @pl.loop(1, SUBS)
    def _(i):
        other = lax.rem(me + i, SUBS)
        pl.semaphore_signal(
            barrier, inc=1, device_id=(other // COLS, lax.rem(other, COLS)), device_id_type=MESH
        )

    pl.semaphore_wait(barrier, SUBS - 1)

    def place(target):
        target_row, target_col = target // COLS, lax.rem(target, COLS)
        rel = lax.rem(target_row // 4 + 4 - heavy, 4)
        light = lax.rem(target_col // 4 + heavy, 2)
        return target_row, target_col, rel, lax.rem(target_row, 4), light, lax.rem(target_col, 4)

    def first_row(rel, t):
        start = jnp.where(rel == 0, t * 128, jnp.where(rel == 2, t * 128 + 96, 512 + t * 64))
        return jnp.where(rel == 3, start + 32, start)

    def parts(target, use):
        target_row, target_col, rel, t, light, u = place(target)
        start = first_row(rel, t)
        for light_row in range(2):
            count = 32 if light_row else 96

            @pl.when((rel != 0) == (light_row == 1))
            def _():
                half = pl.multiple_of(start // 2, 16)
                use(
                    "z",
                    oz.at[target_col, pl.ds(half, count // 2)],
                    count // 2, target_row, target_col,
                )

                @pl.when(light == 0)
                def _():
                    use(
                        "a",
                        oa.at[u, pl.ds(pl.multiple_of(start, 32), count)],
                        count, target_row, target_col,
                    )

                @pl.when(light == 1)
                def _():
                    use(
                        "a",
                        ol.at[u, pl.ds(half, count // 2)],
                        count // 2, target_row, target_col,
                    )

    def box(kind, source, count):
        ref = in_a if kind == "a" else in_z
        return ref.at[pl.ds(pl.multiple_of(source * count, 16), count)]

    def remote(kind, source_ref, count, target_row, target_col):
        send, recv = (send_a, recv_a) if kind == "a" else (send_z, recv_z)
        return pltpu.make_async_remote_copy(
            src_ref=source_ref,
            dst_ref=box(kind, me, count),
            send_sem=send.at[target_row * COLS + target_col],
            recv_sem=recv.at[me],
            device_id=(target_row, target_col),
            device_id_type=MESH,
        )

    def keep(kind, source_ref, count, target_row, target_col):
        copy = pltpu.make_async_copy(source_ref, box(kind, me, count), local_sem)
        copy.start()
        copy.wait()

    def chunk(index):
        return pl.ds(pl.multiple_of(index * 16, 16), 16)

    def corner_part(target):
        return pltpu.make_async_remote_copy(
            src_ref=corner.at[chunk(target)], dst_ref=parts_box.at[chunk(me)],
            send_sem=send_c.at[target], recv_sem=recv_c.at[me],
            device_id=(target // COLS, lax.rem(target, COLS)), device_id_type=MESH,
        )

    def corner_whole(target):
        return pltpu.make_async_remote_copy(
            src_ref=whole_box.at[chunk(me)], dst_ref=whole_box.at[chunk(me)],
            send_sem=send_g.at[target], recv_sem=recv_g.at[me],
            device_id=(target // COLS, lax.rem(target, COLS)), device_id_type=MESH,
        )

    def others(use):
        @pl.loop(1, SUBS)
        def _(i):
            use(lax.rem(me + i, SUBS))

    def landed(box_ref, sem):
        def use(source):
            here = box_ref.at[chunk(source)]
            pltpu.make_async_copy(here, here, sem.at[source]).wait()
        others(use)

    others(lambda target: corner_part(target).start())
    parts_box[chunk(me), :] = corner[chunk(me), :]
    landed(parts_box, recv_c)
    whole_box[chunk(me), :] = lax.fori_loop(
        0, SUBS, lambda i, total: total + parts_box[chunk(i), :], jnp.zeros((16, RUN), F32)
    )
    others(lambda target: corner_whole(target).start())

    @pl.loop(1, SUBS)
    def _(i):
        parts(lax.rem(me + i, SUBS), lambda *a: remote(*a).start())

    parts(me, keep)
    landed(whole_box, recv_g)
    low = lax.broadcasted_iota(jnp.int32, (16, RUN), 1) < 64

    @pl.loop(0, ROWS)
    def _(r):
        top = pl.ds(pl.multiple_of(lax.rem(r, 8) * 64 + r // 8 * SUB, 16), 16)
        bottom = pl.ds(pl.multiple_of(lax.rem(r, 8) * 64 + r // 8 * SUB + 16, 16), 16)
        for w in range(4):
            first = whole_box[chunk(r * COLS + 2 * w), :]
            second = whole_box[chunk(r * COLS + 2 * w + 1), :]
            m_ref[top, w * RUN:(w + 1) * RUN] = jnp.where(low, first, pltpu.roll(second, 64, 1))
            m_ref[bottom, w * RUN:(w + 1) * RUN] = jnp.where(low, pltpu.roll(first, 64, 1), second)

    invert_factor(m_ref, inv_ref, work)

    def arrived(kind, source_ref, count, target_row, target_col):
        recv = recv_a if kind == "a" else recv_z

        @pl.loop(1, SUBS)
        def _(i):
            source = lax.rem(me + i, SUBS)
            here = box(kind, source, count)
            pltpu.make_async_copy(here, here, recv.at[source]).wait()

    parts(me, arrived)

    @pl.loop(1, SUBS)
    def _(i):
        target = lax.rem(me + i, SUBS)
        parts(target, lambda *a: remote(*a).wait_send())
        corner_part(target).wait_send()
        corner_whole(target).wait_send()


def exchange(heavy, corner, oa, ol, oz):
    anywhere = pl.BlockSpec(memory_space=pl.ANY)
    vmem = pl.BlockSpec(memory_space=pltpu.VMEM)
    shape = jax.ShapeDtypeStruct
    return pl.pallas_call(
        functools.partial(exchange_kernel, heavy),
        out_shape=(
            shape((SUBS * 96, RUN), F32), shape((SUBS * 48, RUN), F32), shape((PANEL, PANEL), F32)
        ),
        in_specs=[vmem] + [anywhere] * 3,
        out_specs=(anywhere, anywhere, vmem),
        scratch_shapes=[pltpu.SemaphoreType.DMA((SUBS,))] * 8 + [
            pltpu.SemaphoreType.DMA,
            pltpu.VMEM((SUBS * 16, RUN), F32),
            pltpu.VMEM((SUBS * 16, RUN), F32),
            pltpu.VMEM((PANEL, PANEL), F32),
            pltpu.VMEM((RUN, 2 * RUN), F32),
        ],
        compiler_params=pltpu.CompilerParams(
            collective_id=1 + heavy, has_side_effects=True, vmem_limit_bytes=VMEM_LIMIT // 2
        ),
        name=f"exchange_{heavy}",
    )(corner, oa, ol, oz)


def place_kernel(runs, meta, in_a, in_z, a_ref, z_ref, cols_ref, rows_ref, acc, zacc, ztall):
    rel, light = meta[1], meta[2]
    acc[...] = jnp.zeros_like(acc)
    zacc[...] = jnp.zeros_like(zacc)

    def run(light_row, light_col):
        slots = [jnp.where(rel == 2, 3, jnp.where(rel == 1, 4, 5))] if light_row else [0, 1, 2]
        col_slots = [4, 5] if light_col else [0, 1, 2, 3]
        number = len(slots)
        height = 16 if light_col else SUB
        chunk = chunk_of_lane((height, RUN))

        @pl.loop(0, SUBS)
        def _(s):
            at = [runs[s * 6 + slot] // 4 for slot in slots]
            to = [runs[s * 6 + slot] // 2 for slot in col_slots]
            for p in range(number):
                zrows = pl.ds(pl.multiple_of(at[p] * 16, 16), 16)
                zacc[zrows, :] += in_z[pl.ds(pl.multiple_of((s * number + p) * 16, 16), 16), :]
            for p in range(number):
                piece = in_a[pl.ds(pl.multiple_of((s * number + p) * height, height), height), :]
                new = []
                for q in range(len(to)):
                    tile, place = to[q] // 4, lax.rem(to[q], 4)
                    for half in range(SUB // height):
                        rows = pl.ds(pl.multiple_of(at[p] * SUB + half * height, height), height)
                        moved = pltpu.roll(piece, lax.rem(place + 8 - q - 2 * half, 4) * SUB, 1)
                        moved = jnp.where(chunk == place, moved, 0.0)
                        new.append((q, tile, rows, acc[q, tile, rows, :] + moved))
                for q, tile, rows, value in new:
                    acc[q, tile, rows, :] = value

    for light_row in range(2):
        for light_col in range(2):
            pl.when(((rel != 0) == (light_row == 1)) & (light == light_col))(
                functools.partial(run, light_row, light_col)
            )
    for k in range(8):
        a_ref[:, k * RUN:(k + 1) * RUN] = (acc[0, k] + acc[1, k]) + (acc[2, k] + acc[3, k])
    for k in range(16):
        piece = zacc[k * 16:(k + 1) * 16, :]
        ztall[k * SUB:k * SUB + 16, :] = piece
        ztall[k * SUB + 16:(k + 1) * SUB, :] = pltpu.roll(piece, 64, 1)
    z_ref[...] = ztall[...].T[:64, :]
    cols_ref[...] = a_ref[:, :RUN].T[:64, :]
    rows_ref[:, :1024] = a_ref[:SUB, :]
    rows_ref[:, 1024:] = ztall[:SUB, :]


def place(runs, meta, in_a, in_z):
    smem = pl.BlockSpec(memory_space=pltpu.SMEM)
    vmem = pl.BlockSpec(memory_space=pltpu.VMEM)
    shape = jax.ShapeDtypeStruct
    return pl.pallas_call(
        place_kernel,
        out_shape=(
            shape((512, 1024), F32), shape((64, 512), F32), shape((64, 512), F32), shape((SUB, 1152), F32)
        ),
        in_specs=[smem, smem, vmem, vmem],
        out_specs=(vmem,) * 4,
        scratch_shapes=[
            pltpu.VMEM((4, 8, 512, RUN), F32),
            pltpu.VMEM((256, RUN), F32),
            pltpu.VMEM((512, RUN), F32),
        ],
        compiler_params=pltpu.CompilerParams(vmem_limit_bytes=VMEM_LIMIT),
        name="place",
    )(runs, meta, in_a, in_z)


def panel_kernel(
    a_ref, z_ref, cols_ref, rows_ref, inv_ref, out_ref, zout_ref,
    col_box, row_box, ih, il, lth, ltl, uh, ul, send_c, recv_c, send_r, recv_r,
):
    row, col = lax.axis_index("row"), lax.axis_index("col")
    barrier = pltpu.get_barrier_semaphore()
    peers_c = [lax.rem(col + i, COLS) for i in range(1, COLS)]
    peers_r = [lax.rem(row + i, ROWS) for i in range(1, ROWS)]
    for c in peers_c:
        pl.semaphore_signal(barrier, inc=1, device_id=(row, c), device_id_type=MESH)
    for r in peers_r:
        pl.semaphore_signal(barrier, inc=1, device_id=(r, col), device_id_type=MESH)
    pl.semaphore_wait(barrier, COLS + ROWS - 2)

    def col_place(c):
        return pl.ds(pl.multiple_of(c * 64, 64), 64)

    def row_place(r):
        return pl.ds(pl.multiple_of(lax.rem(r, 8) * 64 + r // 8 * SUB, SUB), SUB)

    sends = [
        pltpu.make_async_remote_copy(
            src_ref=cols_ref, dst_ref=col_box.at[col_place(col)], send_sem=send_c.at[c],
            recv_sem=recv_c.at[col], device_id=(row, c), device_id_type=MESH,
        )
        for c in peers_c
    ] + [
        pltpu.make_async_remote_copy(
            src_ref=rows_ref, dst_ref=row_box.at[row_place(row)], send_sem=send_r.at[r],
            recv_sem=recv_r.at[row], device_id=(r, col), device_id_type=MESH,
        )
        for r in peers_r
    ]
    for send in sends:
        send.start()
    col_box[col_place(col), :] = cols_ref[...]
    row_box[row_place(row), :] = rows_ref[...]
    ih[...], il[...] = split(inv_ref[...])
    for c in peers_c:
        here = col_box.at[col_place(c)]
        pltpu.make_async_copy(here, here, recv_c.at[c]).wait()
    bh, bl = split(col_box[...])
    for i in range(2):
        rows = slice(i * 256, (i + 1) * 256)
        lth[:, rows], ltl[:, rows] = split(dot3(ih[rows, :], il[rows, :], bh, bl).T)
    for r in peers_r:
        here = row_box.at[row_place(r)]
        pltpu.make_async_copy(here, here, recv_r.at[r]).wait()
    for n in range(3):
        cols = slice(n * 384, (n + 1) * 384)
        bh, bl = split(row_box[:, cols])
        uh[:, cols], ul[:, cols] = split(dot3(ih[...], il[...], bh, bl))
    for i in range(2):
        rows = slice(i * 256, (i + 1) * 256)
        for n in range(4):
            cols = slice(n * 256, (n + 1) * 256)
            out_ref[rows, cols] = a_ref[rows, cols] - dot3(lth[rows, :], ltl[rows, :], uh[:, cols], ul[:, cols])
        last = dot3(lth[rows, :], ltl[rows, :], uh[:, 1024:], ul[:, 1024:])
        zout_ref[:, rows] = z_ref[:, rows] - last.T[:64, :]
    for send in sends:
        send.wait_send()


def panel(shifted, modes_local, cols, rows, inverse):
    vmem = pl.BlockSpec(memory_space=pltpu.VMEM)
    shape = jax.ShapeDtypeStruct
    return pl.pallas_call(
        panel_kernel,
        out_shape=(shape((512, 1024), F32), shape((64, 512), F32)),
        in_specs=[vmem] * 5,
        out_specs=(vmem, vmem),
        scratch_shapes=[
            pltpu.VMEM((512, 512), F32), pltpu.VMEM((512, 1152), F32),
            pltpu.VMEM((512, 512), BF16), pltpu.VMEM((512, 512), BF16),
            pltpu.VMEM((512, 512), BF16), pltpu.VMEM((512, 512), BF16),
            pltpu.VMEM((512, 1152), BF16), pltpu.VMEM((512, 1152), BF16),
            pltpu.SemaphoreType.DMA((COLS,)), pltpu.SemaphoreType.DMA((COLS,)),
            pltpu.SemaphoreType.DMA((ROWS,)), pltpu.SemaphoreType.DMA((ROWS,)),
        ],
        compiler_params=pltpu.CompilerParams(
            collective_id=5, has_side_effects=True, vmem_limit_bytes=VMEM_LIMIT // 2
        ),
        name="panel",
    )(shifted, modes_local, cols, rows, inverse)


def slot_order(interface_ids):
    runs = interface_ids[:, ::RUN] // RUN
    kinds = runs % 4
    first = kinds[0]
    heavy = jnp.argmax(jnp.sum(first[None, :] == jnp.arange(4)[:, None], axis=1)).astype(jnp.int32)
    rel = (kinds - heavy) % 4
    key = jnp.where(rel == 1, 2, jnp.where(rel == 2, 1, rel)) * 8 + jnp.arange(6)
    slot = jnp.sum(key[:, None, :] < key[:, :, None], axis=2)
    hit = slot[:, :, None] == jnp.arange(6)
    ordered = jnp.sum(jnp.where(hit, runs[:, :, None], 0), axis=1)
    origin = jnp.sum(jnp.where(hit, jnp.arange(6)[None, :, None], 0), axis=1)
    return heavy, ordered.astype(jnp.int32), origin.astype(jnp.int32)


def body(
    inverse_factor,
    coupling,
    boundary_stiffness,
    interior_mass,
    boundary_mass,
    interface_ids,
    trial_modes,
):
    row, col = lax.axis_index("row"), lax.axis_index("col")
    heavy, ordered, origin = slot_order(interface_ids)
    me = row * COLS + col
    own = lax.dynamic_index_in_dim(ordered, me, 0, keepdims=False)
    first = jnp.arange(4)[:, None] == own[None, :]
    held = jnp.sum(jnp.where(first, jnp.arange(6)[None, :] + 1, 0), axis=1) - 1
    perm = jnp.concatenate([lax.dynamic_index_in_dim(origin, me, 0, keepdims=False), held]).astype(jnp.int32)
    runs = ordered.reshape(-1)
    meta = jnp.stack([row, (row // 4 + 4 - heavy) % 4, (col // 4 + heavy) % 2, heavy % 2]).astype(jnp.int32)
    sent = modes_pack(runs, meta, trial_modes)
    modes = lax.all_to_all(sent, "col", split_axis=0, concat_axis=0, tiled=True)
    oa, ol, chi, clo, corner = condense(
        perm, inverse_factor[0], coupling[0], boundary_stiffness[0], interior_mass, boundary_mass
    )
    oz = products(meta, chi, clo, modes)
    in_a, in_z, inverse = lax.switch(
        heavy, [functools.partial(exchange, h) for h in range(4)], corner, oa, ol, oz
    )
    shifted, modes_local, cols, rows = place(runs, meta, in_a, in_z)
    return panel(shifted, modes_local, cols, rows, inverse)


def solution(mesh):
    return jax.shard_map(
        body,
        mesh=mesh,
        in_specs=(
            P(("row", "col"), None, None),
            P(("row", "col"), None, None),
            P(("row", "col"), None, None),
            P(("row", "col"), None),
            P(("row", "col"), None),
            P(),
            P("col", None),
        ),
        out_specs=(P("row", "col"), P("col", "row")),
        check_vma=False,
    )
```

```python
import functools

import jax
import jax.numpy as jnp
from jax import lax
from jax.experimental import pallas as pl
from jax.experimental.pallas import tpu as pltpu
from jax.sharding import PartitionSpec as P

SUB = 32
RUN = 128
NG = 8192
PANEL = 512
NI = 1024
NB = 768
ROWS = 16
COLS = 8
SUBS = ROWS * COLS
MODES = 512
SHIFT = 0.05
F32 = jnp.float32
BF16 = jnp.bfloat16
MESH = pl.DeviceIdType.MESH
VMEM_LIMIT = 60 * 1024 * 1024

high = lax.Precision.HIGH
highest = lax.Precision.HIGHEST


def split(x):
    hi = x.astype(BF16)
    return hi, (x - hi.astype(F32)).astype(BF16)


def dot(a, b):
    return jnp.dot(a, b, preferred_element_type=F32)


def dot3(ah, al, bh, bl):
    return dot(ah, bh) + (dot(ah, bl) + dot(al, bh))


def chunk_of_lane(shape):
    return lax.broadcasted_iota(jnp.int32, shape, 1) // SUB


def gather_chunks(tiles, picks, chunk):
    out = None
    for place, (tile, source) in enumerate(picks):
        amount = (place - source) * SUB % RUN
        moved = pltpu.roll(tiles[tile], amount, 1) if amount else tiles[tile]
        out = moved if out is None else jnp.where(chunk == place, moved, out)
    return out


def permute_tiles(tiles):
    chunk = chunk_of_lane(tiles[0].shape)
    out = [gather_chunks(tiles, [(q, u) for q in range(4)], chunk) for u in range(4)]
    for w in range(2):
        out.append(gather_chunks(tiles, [(4 + k % 2, 2 * w + k // 2) for k in range(4)], chunk))
    return out


def pack_half(x, odd):
    low = lax.broadcasted_iota(jnp.int32, (16, RUN), 1) < 64
    top, bottom = x[:16], x[16:]
    if odd:
        return jnp.where(low, pltpu.roll(top, 64, 1), bottom)
    return jnp.where(low, top, pltpu.roll(bottom, 64, 1))


def condense_kernel(
    perm, f_ref, c_ref, b_ref, im_ref, bm_ref,
    oa_ref, ol_ref, chi_ref, clo_ref,
    cph, cpl, fh, fl, fth, ftl, wh, wl, wth, wtl, bp, bmp,
):
    def slot_cols(slot):
        return pl.ds(pl.multiple_of(perm[slot] * RUN, RUN), RUN)

    @pl.loop(0, NI // 32)
    def _(i):
        rows = pl.ds(pl.multiple_of(i * 32, 32), 32)
        out = permute_tiles([c_ref[rows, slot_cols(s)] for s in range(6)])
        for k in range(6):
            hi, lo = split(out[k])
            cph[rows, k * RUN:(k + 1) * RUN] = hi
            cpl[rows, k * RUN:(k + 1) * RUN] = lo

    out = permute_tiles([bm_ref[:, slot_cols(s)] for s in range(6)])
    for k in range(6):
        bmp[:, k * RUN:(k + 1) * RUN] = out[k]

    def permute_rows(slot, u, place):
        rows = pl.ds(pl.multiple_of(perm[slot] * RUN + u * SUB, SUB), SUB)
        target = pl.ds(pl.multiple_of(place, SUB), SUB)
        out = permute_tiles([b_ref[rows, slot_cols(s)] for s in range(6)])
        for k in range(6):
            bp[target, k * RUN:(k + 1) * RUN] = out[k]

    @pl.loop(0, 4)
    def _(u):
        for q in range(4):
            permute_rows(q, u, (u * 4 + q) * SUB)
        for q in range(2):
            permute_rows(4 + q, u, 512 + (u * 2 + q) * SUB)

    root = jnp.sqrt(im_ref[...])
    for i in range(4):
        rows = slice(i * 256, (i + 1) * 256)
        for j in range(i + 1):
            cols = slice(j * 256, (j + 1) * 256)
            block = f_ref[rows, cols]
            fh[rows, cols], fl[rows, cols] = split(block)
            fth[cols, rows], ftl[cols, rows] = split((block * root[:, cols]).T)
    for i in range(4):
        rows = slice(i * 256, (i + 1) * 256)
        depth = (i + 1) * 256
        for n in range(3):
            cols = slice(n * 256, (n + 1) * 256)
            w = dot3(fh[rows, :depth], fl[rows, :depth], cph[:depth, cols], cpl[:depth, cols])
            wh[rows, cols], wl[rows, cols] = split(w)
            wth[cols, rows], wtl[cols, rows] = split(w.T)
    for j in range(3):
        rows = slice(j * 256, (j + 1) * 256)
        for n in range(j, 3):
            cols = slice(n * 256, (n + 1) * 256)
            gram = dot3(wth[rows, :], wtl[rows, :], wh[:, cols], wl[:, cols])
            bp[rows, cols] = bp[rows, cols] - gram
    for i in range(4):
        rows = slice(i * 256, (i + 1) * 256)
        start = i * 256
        for n in range(3):
            cols = slice(n * 256, (n + 1) * 256)
            phi = dot3(fth[rows, start:], ftl[rows, start:], wh[start:, cols], wl[start:, cols])
            cph[rows, cols], cpl[rows, cols] = split(phi)
            wth[cols, rows], wtl[cols, rows] = split(phi.T)

    def put(rows, n, value):
        for half in range(2):
            tile = 2 * n + half
            part = value[:, half * RUN:(half + 1) * RUN]
            if tile < 4:
                oa_ref[tile, rows, :] = part
            else:
                for k in range(8):
                    start = (rows.start + k * SUB) // 2
                    for odd in range(2):
                        ol_ref[2 * (tile - 4) + odd, start:start + 16, :] = pack_half(
                            part[k * SUB:(k + 1) * SUB], odd
                        )

    for j in range(3):
        rows = slice(j * 256, (j + 1) * 256)
        for n in range(j, 3):
            cols = slice(n * 256, (n + 1) * 256)
            mass = dot3(wth[rows, :], wtl[rows, :], cph[:, cols], cpl[:, cols])
            if n == j:
                here = lax.broadcasted_iota(jnp.int32, (256, 256), 0)
                there = lax.broadcasted_iota(jnp.int32, (256, 256), 1)
                mass = mass + jnp.where(here == there, bmp[:, cols], 0.0)
            value = bp[rows, cols] - SHIFT * mass
            chi_ref[rows, cols], clo_ref[rows, cols] = split(mass)
            put(rows, n, value)
            if n != j:
                chi_ref[cols, rows], clo_ref[cols, rows] = split(mass.T)
                put(cols, j, value.T)


def condense(perm, factor, link, stiff, inner, outer):
    vmem = pl.BlockSpec(memory_space=pltpu.VMEM)
    shape = jax.ShapeDtypeStruct
    return pl.pallas_call(
        condense_kernel,
        out_shape=(
            shape((4, NB, RUN), F32),
            shape((4, NB // 2, RUN), F32),
            shape((NB, NB), BF16),
            shape((NB, NB), BF16),
        ),
        in_specs=[pl.BlockSpec(memory_space=pltpu.SMEM)] + [vmem] * 5,
        out_specs=(vmem,) * 4,
        scratch_shapes=[
            pltpu.VMEM((NI, NB), BF16), pltpu.VMEM((NI, NB), BF16),
            pltpu.VMEM((NI, NI), BF16), pltpu.VMEM((NI, NI), BF16),
            pltpu.VMEM((NI, NI), BF16), pltpu.VMEM((NI, NI), BF16),
            pltpu.VMEM((NI, NB), BF16), pltpu.VMEM((NI, NB), BF16),
            pltpu.VMEM((NB, NI), BF16), pltpu.VMEM((NB, NI), BF16),
            pltpu.VMEM((NB, NB), F32), pltpu.VMEM((1, NB), F32),
        ],
        compiler_params=pltpu.CompilerParams(vmem_limit_bytes=VMEM_LIMIT),
        cost_estimate=pl.CostEstimate(flops=11 * 10**9, bytes_accessed=16 * 10**6, transcendentals=0),
        name="condense",
    )(perm, factor, link, stiff, inner, outer)


def modes_pack_kernel(runs, meta, q_ref, out_ref):
    light = meta[2]
    for c in range(COLS):
        for q in range(4):
            slot = jnp.where(light == 1, 4 + min(q, 1), q)
            block = runs[(meta[0] * COLS + c) * 6 + slot] // 2
            out_ref[c, q * SUB:(q + 1) * SUB, :] = q_ref[pl.ds(pl.multiple_of(block * SUB, SUB), SUB), :]


def modes_pack(runs, meta, modes):
    smem = pl.BlockSpec(memory_space=pltpu.SMEM)
    vmem = pl.BlockSpec(memory_space=pltpu.VMEM)
    return pl.pallas_call(
        modes_pack_kernel,
        out_shape=jax.ShapeDtypeStruct((COLS, RUN, MODES), F32),
        in_specs=[smem, smem, vmem],
        out_specs=vmem,
        compiler_params=pltpu.CompilerParams(vmem_limit_bytes=VMEM_LIMIT),
        name="modes_pack",
    )(runs, meta, modes)


def multiply_modes(parity, chi_ref, clo_ref, q_ref, out_ref, qh, ql):
    for u in range(4):
        block = q_ref[parity * 4 + u]
        rows = slice(u * RUN, (u + 1) * RUN)
        qh[rows, :], ql[rows, :] = split(block)
        block = q_ref[(1 - parity) * 4 + u, :64, :]
        rows = slice(512 + u * 64, 512 + (u + 1) * 64)
        qh[rows, :], ql[rows, :] = split(block)
    for j in range(3):
        rows = slice(j * 256, (j + 1) * 256)
        for n in range(2):
            cols = slice(n * 256, (n + 1) * 256)
            z = dot3(chi_ref[rows, :], clo_ref[rows, :], qh[:, cols], ql[:, cols])
            for half in range(2):
                for k in range(8):
                    start = (j * 256 + k * SUB) // 2
                    part = z[k * SUB:(k + 1) * SUB, half * RUN:(half + 1) * RUN]
                    for odd in range(2):
                        out_ref[n * 4 + half * 2 + odd, start:start + 16, :] = pack_half(part, odd)


def eye(n):
    return jnp.where(
        lax.broadcasted_iota(jnp.int32, (n, n), 0) == lax.broadcasted_iota(jnp.int32, (n, n), 1), 1.0, 0.0
    )


def exact(a, b, axis=1):
    return lax.dot_general(
        a, b, (((axis,), (0,)), ((), ())), precision=highest, preferred_element_type=F32
    )


STRIP = 16
STRIDE = 37


def invert_factor(m_ref, inv_ref, work, before_last):
    inv_ref[...] = jnp.zeros_like(inv_ref)
    lane = lax.broadcasted_iota(jnp.int32, (1, RUN), 1)
    height = lax.broadcasted_iota(jnp.int32, (STRIP, 1), 0)
    for k in range(4):
        if k == 3:
            before_last()
        block = slice(k * RUN, (k + 1) * RUN)
        work[:, :RUN] = m_ref[block, block]
        work[:, RUN:] = eye(RUN)

        @pl.loop(0, RUN // STRIP)
        def _(group):
            start = pl.multiple_of(group * STRIP, STRIP)
            strip = work[pl.ds(start, STRIP), :]
            square = strip[:, :RUN]
            columns = [
                jnp.sum(jnp.where(lane == start + j, square, 0.0), axis=1, keepdims=True)
                for j in range(STRIP)
            ]
            for j in range(STRIP):
                scale = lax.rsqrt(columns[j][j:j + 1])
                lead = strip[j:j + 1] * scale
                factor = jnp.where(height > j, columns[j] * scale, 0.0)
                strip = jnp.where(height == j, lead, strip - factor * lead)
                for k2 in range(j + 1, STRIP):
                    columns[k2] = columns[k2] - factor * (columns[k2][j:j + 1] * scale)
            later = jnp.where(lane >= start + STRIP, strip[:, :RUN], 0.0)
            work[...] = work[...] - exact(later, strip, 0)
            work[pl.ds(start, STRIP), :] = strip

        t = work[:, RUN:]
        left = None
        if k:
            left = exact(t, inv_ref[block, :k * RUN])
            inv_ref[block, :k * RUN] = left
        inv_ref[block, block] = t
        if k < 3:
            x = exact(t, m_ref[block, (k + 1) * RUN:])
            below = slice((k + 1) * RUN, 512)
            m_ref[below, below] = m_ref[below, below] - exact(x, x, 0)
            if k:
                inv_ref[below, :k * RUN] = inv_ref[below, :k * RUN] - exact(x, left, 0)
            inv_ref[below, block] = inv_ref[below, block] - exact(x, t, 0)


def exchange_kernel(
    heavy, oa, ol, chi, clo, modes, in_a, in_z,
    send_a, recv_a, send_z, recv_z, local_sem, oz, qh, ql,
):
    row, col = lax.axis_index("row"), lax.axis_index("col")
    me = row * COLS + col
    barrier = pltpu.get_barrier_semaphore()

    @pl.loop(1, SUBS)
    def _(i):
        other = lax.rem(me + i, SUBS)
        pl.semaphore_signal(
            barrier, inc=1, device_id=(other // COLS, lax.rem(other, COLS)), device_id_type=MESH
        )

    pl.semaphore_wait(barrier, SUBS - 1)

    def place(target):
        target_row, target_col = target // COLS, lax.rem(target, COLS)
        rel = lax.rem(target_row // 4 + 4 - heavy, 4)
        light = lax.rem(target_col // 4 + heavy, 2)
        return target_row, target_col, rel, lax.rem(target_row, 4), light, lax.rem(target_col, 4)

    def first_row(rel, t):
        start = jnp.where(rel == 0, t * 128, jnp.where(rel == 2, t * 128 + 96, 512 + t * 64))
        return jnp.where(rel == 3, start + 32, start)

    def parts(target, use):
        target_row, target_col, rel, t, light, u = place(target)
        start = first_row(rel, t)
        for light_row in range(2):
            count = 32 if light_row else 96

            @pl.when((rel != 0) == (light_row == 1))
            def _():
                half = pl.multiple_of(start // 2, 16)
                use(
                    "z",
                    oz.at[target_col, pl.ds(half, count // 2)],
                    count // 2, target_row, target_col,
                )

                @pl.when(light == 0)
                def _():
                    use(
                        "a",
                        oa.at[u, pl.ds(pl.multiple_of(start, 32), count)],
                        count, target_row, target_col,
                    )

                @pl.when(light == 1)
                def _():
                    use(
                        "a",
                        ol.at[u, pl.ds(half, count // 2)],
                        count // 2, target_row, target_col,
                    )

    def box(kind, source, count):
        ref = in_a if kind == "a" else in_z
        return ref.at[pl.ds(pl.multiple_of(source * count, 16), count)]

    def remote(kind, source_ref, count, target_row, target_col):
        send, recv = (send_a, recv_a) if kind == "a" else (send_z, recv_z)
        return pltpu.make_async_remote_copy(
            src_ref=source_ref,
            dst_ref=box(kind, me, count),
            send_sem=send.at[target_row * COLS + target_col],
            recv_sem=recv.at[me],
            device_id=(target_row, target_col),
            device_id_type=MESH,
        )

    def keep(kind, source_ref, count, target_row, target_col):
        copy = pltpu.make_async_copy(source_ref, box(kind, me, count), local_sem)
        copy.start()
        copy.wait()

    def only(wanted, use):
        def chosen(kind, *a):
            if kind == wanted:
                use(kind, *a)
        return chosen

    def send_blocks(kind):
        @pl.loop(1, SUBS)
        def _(i):
            parts(lax.rem(me + i * STRIDE, SUBS), only(kind, lambda *a: remote(*a).start()))

    send_blocks("a")
    multiply_modes(heavy % 2, chi, clo, modes, oz, qh, ql)
    send_blocks("z")
    parts(me, keep)

    def arrived(kind, source_ref, count, target_row, target_col):
        recv = recv_a if kind == "a" else recv_z

        @pl.loop(1, SUBS)
        def _(i):
            source = lax.rem(me + i, SUBS)
            here = box(kind, source, count)
            pltpu.make_async_copy(here, here, recv.at[source]).wait()

    parts(me, arrived)

    @pl.loop(1, SUBS)
    def _(i):
        target = lax.rem(me + i, SUBS)
        parts(target, lambda *a: remote(*a).wait_send())


def exchange(heavy, oa, ol, chi, clo, modes):
    anywhere = pl.BlockSpec(memory_space=pl.ANY)
    vmem = pl.BlockSpec(memory_space=pltpu.VMEM)
    shape = jax.ShapeDtypeStruct
    return pl.pallas_call(
        functools.partial(exchange_kernel, heavy),
        out_shape=(shape((SUBS * 96, RUN), F32), shape((SUBS * 48, RUN), F32)),
        in_specs=[anywhere] * 2 + [vmem] * 3,
        out_specs=(anywhere, anywhere),
        scratch_shapes=[pltpu.SemaphoreType.DMA((SUBS,))] * 4 + [
            pltpu.SemaphoreType.DMA,
            pltpu.VMEM((COLS, NB // 2, RUN), F32),
            pltpu.VMEM((NB, MODES), BF16),
            pltpu.VMEM((NB, MODES), BF16),
        ],
        compiler_params=pltpu.CompilerParams(
            collective_id=1 + heavy, has_side_effects=True, vmem_limit_bytes=VMEM_LIMIT
        ),
        name=f"exchange_{heavy}",
    )(oa, ol, chi, clo, modes)


def place_kernel(
    runs, meta, a_hbm, z_hbm, a_ref, z_ref, cols_ref, rows_ref, piece_ref, in_a, in_z, acc, zacc, ztall, sem
):
    rel, light = meta[1], meta[2]
    group = SUBS // 8

    def run(light_row, light_col):
        slots = [jnp.where(rel == 2, 3, jnp.where(rel == 1, 4, 5))] if light_row else [0, 1, 2]
        col_slots = [4, 5] if light_col else [0, 1, 2, 3]
        number = len(slots)
        height = 16 if light_col else SUB
        chunk = chunk_of_lane((height, RUN))

        def copies(g):
            a_rows = pl.ds(pl.multiple_of(g * group * number * height, 128), group * number * height)
            z_rows = pl.ds(pl.multiple_of(g * group * number * 16, 128), group * number * 16)
            return (
                pltpu.make_async_copy(a_hbm.at[a_rows], in_a.at[a_rows], sem.at[g, 0]),
                pltpu.make_async_copy(z_hbm.at[z_rows], in_z.at[z_rows], sem.at[g, 1]),
            )

        for g in range(8):
            for copy in copies(g):
                copy.start()
        acc[...] = jnp.zeros_like(acc)
        zacc[...] = jnp.zeros_like(zacc)

        def one(s):
            at = [runs[s * 6 + slot] // 4 for slot in slots]
            to = [runs[s * 6 + slot] // 2 for slot in col_slots]
            for p in range(number):
                zrows = pl.ds(pl.multiple_of(at[p] * 16, 16), 16)
                zacc[zrows, :] += in_z[pl.ds(pl.multiple_of((s * number + p) * 16, 16), 16), :]
            for p in range(number):
                piece = in_a[pl.ds(pl.multiple_of((s * number + p) * height, height), height), :]
                new = []
                for q in range(len(to)):
                    tile, place = to[q] // 4, lax.rem(to[q], 4)
                    for half in range(SUB // height):
                        rows = pl.ds(pl.multiple_of(at[p] * SUB + half * height, height), height)
                        moved = pltpu.roll(piece, lax.rem(place + 8 - q - 2 * half, 4) * SUB, 1)
                        moved = jnp.where(chunk == place, moved, 0.0)
                        new.append((q, tile, rows, acc[q, tile, rows, :] + moved))
                for q, tile, rows, value in new:
                    acc[q, tile, rows, :] = value

        @pl.loop(0, 8)
        def _(g):
            for copy in copies(g):
                copy.wait()

            @pl.loop(0, group, unroll=4)
            def _(i):
                one(g * group + i)

    for light_row in range(2):
        for light_col in range(2):
            pl.when(((rel != 0) == (light_row == 1)) & (light == light_col))(
                functools.partial(run, light_row, light_col)
            )
    for k in range(8):
        a_ref[:, k * RUN:(k + 1) * RUN] = (acc[0, k] + acc[1, k]) + (acc[2, k] + acc[3, k])
    for k in range(16):
        piece = zacc[k * 16:(k + 1) * 16, :]
        ztall[k * SUB:k * SUB + 16, :] = piece
        ztall[k * SUB + 16:(k + 1) * SUB, :] = pltpu.roll(piece, 64, 1)
    z_ref[...] = ztall[...].T[:64, :]
    cols_ref[...] = a_ref[:, :RUN].T[:64, :]
    piece_ref[...] = cols_ref[:, :RUN]
    rows_ref[:, :1024] = a_ref[:SUB, :]
    rows_ref[:, 1024:] = ztall[:SUB, :]


def place(runs, meta, in_a, in_z):
    smem = pl.BlockSpec(memory_space=pltpu.SMEM)
    vmem = pl.BlockSpec(memory_space=pltpu.VMEM)
    shape = jax.ShapeDtypeStruct
    return pl.pallas_call(
        place_kernel,
        out_shape=(
            shape((512, 1024), F32), shape((64, 512), F32), shape((64, 512), F32), shape((SUB, 1152), F32),
            shape((64, RUN), F32),
        ),
        in_specs=[smem, smem] + [pl.BlockSpec(memory_space=pl.ANY)] * 2,
        out_specs=(vmem,) * 5,
        scratch_shapes=[
            pltpu.VMEM((SUBS * 96, RUN), F32),
            pltpu.VMEM((SUBS * 48, RUN), F32),
            pltpu.VMEM((4, 8, 512, RUN), F32),
            pltpu.VMEM((256, RUN), F32),
            pltpu.VMEM((512, RUN), F32),
            pltpu.SemaphoreType.DMA((8, 2)),
        ],
        compiler_params=pltpu.CompilerParams(vmem_limit_bytes=VMEM_LIMIT),
        name="place",
    )(runs, meta, in_a, in_z)


def panel_kernel(
    a_hbm, z_hbm, cols_ref, rows_ref, piece_ref, out_ref, zout_ref,
    a_ref, z_ref, col_box, row_box, ih, il, lth, ltl, uh, ul, inv_ref, m_ref, work, strips, mine,
    send_c, recv_c, send_r, recv_r, send_f, local_sem, send_p, recv_p, send_m, recv_m, send_n,
):
    row, col = lax.axis_index("row"), lax.axis_index("col")
    barrier = pltpu.get_barrier_semaphore()
    peers_c = [lax.rem(col + i, COLS) for i in (1, 7, 2, 6, 3, 5, 4)]
    peers_r = [lax.rem(row + 2 * i, ROWS) for i in (1, 7, 2, 6, 3, 5, 4)]
    partner = row + 1 - 2 * lax.rem(row, 2)
    for c in peers_c:
        pl.semaphore_signal(barrier, inc=1, device_id=(row, c), device_id_type=MESH)
    for r in peers_r + [partner]:
        pl.semaphore_signal(barrier, inc=1, device_id=(r, col), device_id_type=MESH)
    pl.semaphore_wait(barrier, 15)

    def col_place(c):
        return pl.ds(pl.multiple_of(c * 64, 64), 64)

    def row_place(r):
        return pl.ds(pl.multiple_of(lax.rem(r, 8) * 64 + r // 8 * SUB, SUB), SUB)

    sends = [
        pltpu.make_async_remote_copy(
            src_ref=piece_ref, dst_ref=strips.at[col_place(col)], send_sem=send_p.at[c],
            recv_sem=recv_p.at[col], device_id=(row, c), device_id_type=MESH,
        )
        for c in peers_c
    ]
    for send in sends:
        send.start()
    locals_ = [
        pltpu.make_async_copy(cols_ref, col_box.at[col_place(col)], local_sem.at[0]),
        pltpu.make_async_copy(rows_ref, row_box.at[row_place(row)], local_sem.at[1]),
        pltpu.make_async_copy(a_hbm, a_ref, local_sem.at[2]),
        pltpu.make_async_copy(z_hbm, z_ref, local_sem.at[3]),
    ]
    for copy in locals_:
        copy.start()
    strips[col_place(col), :] = piece_ref[...]
    for c in peers_c:
        here = strips.at[col_place(c)]
        pltpu.make_async_copy(here, here, recv_p.at[c]).wait()
    mine[...] = strips[...].T[:SUB, :]

    def gather_rows(source_ref, box, send, recv, again):
        def copy(ref, r, sem, origin):
            return pltpu.make_async_remote_copy(
                src_ref=ref, dst_ref=box.at[row_place(origin)], send_sem=sem.at[r],
                recv_sem=recv.at[origin], device_id=(r, col), device_id_type=MESH,
            )

        first = [copy(source_ref, r, send, row) for r in peers_r + [partner]]
        handed = []

        def forward():
            for r in peers_r:
                here = box.at[row_place(r)]
                pltpu.make_async_copy(here, here, recv.at[r]).wait()
                onward = pltpu.make_async_remote_copy(
                    src_ref=here, dst_ref=here, send_sem=again.at[r],
                    recv_sem=recv.at[r], device_id=(partner, col), device_id_type=MESH,
                )
                onward.start()
                handed.append(onward)

        def finish():
            for r in [partner] + [lax.rem(partner + 2 * i, ROWS) for i in (1, 7, 2, 6, 3, 5, 4)]:
                here = box.at[row_place(r)]
                pltpu.make_async_copy(here, here, recv.at[r]).wait()

        def drained():
            for onward in handed:
                onward.wait_send()

        for send_one in first:
            send_one.start()
        sends.extend(first)
        return forward, finish, drained

    forward, finish, drained = gather_rows(mine, m_ref, send_m, recv_m, send_n)
    m_ref[row_place(row), :] = mine[...]
    forward()
    col_sends = [
        pltpu.make_async_remote_copy(
            src_ref=cols_ref, dst_ref=col_box.at[col_place(col)], send_sem=send_c.at[c],
            recv_sem=recv_c.at[col], device_id=(row, c), device_id_type=MESH,
        )
        for c in peers_c
    ]
    forward_rows, finish_rows, drained_rows = gather_rows(rows_ref, row_box, send_r, recv_r, send_f)
    for send in col_sends:
        send.start()
    sends.extend(col_sends)
    finish()
    drained()
    invert_factor(m_ref, inv_ref, work, forward_rows)
    ih[...], il[...] = split(inv_ref[...])
    for copy in locals_:
        copy.wait()
    for c in peers_c:
        here = col_box.at[col_place(c)]
        pltpu.make_async_copy(here, here, recv_c.at[c]).wait()
    bh, bl = split(col_box[...])
    for i in range(2):
        rows = slice(i * 256, (i + 1) * 256)
        lth[:, rows], ltl[:, rows] = split(dot3(ih[rows, :], il[rows, :], bh, bl).T)
    finish_rows()
    for n in range(3):
        cols = slice(n * 384, (n + 1) * 384)
        bh, bl = split(row_box[:, cols])
        uh[:, cols], ul[:, cols] = split(dot3(ih[...], il[...], bh, bl))
    for i in range(2):
        rows = slice(i * 256, (i + 1) * 256)
        for n in range(4):
            cols = slice(n * 256, (n + 1) * 256)
            out_ref[rows, cols] = a_ref[rows, cols] - dot3(lth[rows, :], ltl[rows, :], uh[:, cols], ul[:, cols])
        last = dot3(lth[rows, :], ltl[rows, :], uh[:, 1024:], ul[:, 1024:])
        zout_ref[:, rows] = z_ref[:, rows] - last.T[:64, :]
    drained_rows()
    for send in sends:
        send.wait_send()


def panel(shifted, modes_local, cols, rows, piece):
    vmem = pl.BlockSpec(memory_space=pltpu.VMEM)
    anywhere = pl.BlockSpec(memory_space=pl.ANY)
    shape = jax.ShapeDtypeStruct
    return pl.pallas_call(
        panel_kernel,
        out_shape=(shape((512, 1024), F32), shape((64, 512), F32)),
        in_specs=[anywhere] * 4 + [vmem],
        out_specs=(vmem, vmem),
        scratch_shapes=[
            pltpu.VMEM((512, 1024), F32), pltpu.VMEM((64, 512), F32),
            pltpu.VMEM((512, 512), F32), pltpu.VMEM((512, 1152), F32),
            pltpu.VMEM((512, 512), BF16), pltpu.VMEM((512, 512), BF16),
            pltpu.VMEM((512, 512), BF16), pltpu.VMEM((512, 512), BF16),
            pltpu.VMEM((512, 1152), BF16), pltpu.VMEM((512, 1152), BF16),
            pltpu.VMEM((PANEL, PANEL), F32), pltpu.VMEM((PANEL, PANEL), F32),
            pltpu.VMEM((RUN, 2 * RUN), F32), pltpu.VMEM((PANEL, RUN), F32), pltpu.VMEM((SUB, PANEL), F32),
            pltpu.SemaphoreType.DMA((COLS,)), pltpu.SemaphoreType.DMA((COLS,)),
            pltpu.SemaphoreType.DMA((ROWS,)), pltpu.SemaphoreType.DMA((ROWS,)),
            pltpu.SemaphoreType.DMA((ROWS,)), pltpu.SemaphoreType.DMA((4,)),
            pltpu.SemaphoreType.DMA((COLS,)), pltpu.SemaphoreType.DMA((COLS,)),
            pltpu.SemaphoreType.DMA((ROWS,)), pltpu.SemaphoreType.DMA((ROWS,)),
            pltpu.SemaphoreType.DMA((ROWS,)),
        ],
        compiler_params=pltpu.CompilerParams(
            collective_id=5, has_side_effects=True, vmem_limit_bytes=VMEM_LIMIT
        ),
        name="panel",
    )(shifted, modes_local, cols, rows, piece)


def slot_order(interface_ids):
    runs = interface_ids[:, ::RUN] // RUN
    kinds = runs % 4
    first = kinds[0]
    heavy = jnp.argmax(jnp.sum(first[None, :] == jnp.arange(4)[:, None], axis=1)).astype(jnp.int32)
    rel = (kinds - heavy) % 4
    key = jnp.where(rel == 1, 2, jnp.where(rel == 2, 1, rel)) * 8 + jnp.arange(6)
    slot = jnp.sum(key[:, None, :] < key[:, :, None], axis=2)
    hit = slot[:, :, None] == jnp.arange(6)
    ordered = jnp.sum(jnp.where(hit, runs[:, :, None], 0), axis=1)
    origin = jnp.sum(jnp.where(hit, jnp.arange(6)[None, :, None], 0), axis=1)
    return heavy, ordered.astype(jnp.int32), origin.astype(jnp.int32)


def body(
    inverse_factor,
    coupling,
    boundary_stiffness,
    interior_mass,
    boundary_mass,
    interface_ids,
    trial_modes,
):
    row, col = lax.axis_index("row"), lax.axis_index("col")
    heavy, ordered, origin = slot_order(interface_ids)
    me = row * COLS + col
    perm = lax.dynamic_index_in_dim(origin, me, 0, keepdims=False)
    runs = ordered.reshape(-1)
    meta = jnp.stack([row, (row // 4 + 4 - heavy) % 4, (col // 4 + heavy) % 2]).astype(jnp.int32)
    sent = modes_pack(runs, meta, trial_modes)
    modes = lax.all_to_all(sent, "col", split_axis=0, concat_axis=0, tiled=True)
    oa, ol, chi, clo = condense(
        perm, inverse_factor[0], coupling[0], boundary_stiffness[0], interior_mass, boundary_mass
    )
    in_a, in_z = lax.switch(
        heavy, [functools.partial(exchange, h) for h in range(4)], oa, ol, chi, clo, modes
    )
    shifted, modes_local, cols, rows, piece = place(runs, meta, in_a, in_z)
    return panel(shifted, modes_local, cols, rows, piece)


def solution(mesh):
    return jax.shard_map(
        body,
        mesh=mesh,
        in_specs=(
            P(("row", "col"), None, None),
            P(("row", "col"), None, None),
            P(("row", "col"), None, None),
            P(("row", "col"), None),
            P(("row", "col"), None),
            P(),
            P("col", None),
        ),
        out_specs=(P("row", "col"), P("col", "row")),
        check_vma=False,
    )
```

```python
import functools

import jax
import jax.numpy as jnp
from jax import lax
from jax.experimental import pallas as pl
from jax.experimental.pallas import tpu as pltpu
from jax.sharding import PartitionSpec as P

SUB = 32
RUN = 128
NG = 8192
PANEL = 512
NI = 1024
NB = 768
ROWS = 16
COLS = 8
SUBS = ROWS * COLS
MODES = 512
SHIFT = 0.05
F32 = jnp.float32
BF16 = jnp.bfloat16
MESH = pl.DeviceIdType.MESH
VMEM_LIMIT = 60 * 1024 * 1024

high = lax.Precision.HIGH
highest = lax.Precision.HIGHEST


def split(x):
    hi = x.astype(BF16)
    return hi, (x - hi.astype(F32)).astype(BF16)


def dot(a, b):
    return jnp.dot(a, b, preferred_element_type=F32)


def dot3(ah, al, bh, bl):
    return dot(ah, bh) + (dot(ah, bl) + dot(al, bh))


def chunk_of_lane(shape):
    return lax.broadcasted_iota(jnp.int32, shape, 1) // SUB


def gather_chunks(tiles, picks, chunk):
    out = None
    for place, (tile, source) in enumerate(picks):
        amount = (place - source) * SUB % RUN
        moved = pltpu.roll(tiles[tile], amount, 1) if amount else tiles[tile]
        out = moved if out is None else jnp.where(chunk == place, moved, out)
    return out


def permute_tiles(tiles):
    chunk = chunk_of_lane(tiles[0].shape)
    out = [gather_chunks(tiles, [(q, u) for q in range(4)], chunk) for u in range(4)]
    for w in range(2):
        out.append(gather_chunks(tiles, [(4 + k % 2, 2 * w + k // 2) for k in range(4)], chunk))
    return out


def pack_half(x, odd):
    low = lax.broadcasted_iota(jnp.int32, (16, RUN), 1) < 64
    top, bottom = x[:16], x[16:]
    if odd:
        return jnp.where(low, pltpu.roll(top, 64, 1), bottom)
    return jnp.where(low, top, pltpu.roll(bottom, 64, 1))


def condense_kernel(
    perm, f_hbm, c_hbm, b_hbm, im_ref, bm_ref,
    oa_ref, ol_ref, chi_ref, clo_ref,
    cph, cpl, fh, fl, fth, ftl, wh, wl, wth, wtl, bp, bmp,
    f_ref, c_ref, b_ref, sem,
):
    loads = [
        pltpu.make_async_copy(source, target, sem.at[k])
        for k, (source, target) in enumerate(((c_hbm, c_ref), (b_hbm, b_ref), (f_hbm, f_ref)))
    ]
    for load in loads:
        load.start()

    def slot_cols(slot):
        return pl.ds(pl.multiple_of(perm[slot] * RUN, RUN), RUN)

    loads[0].wait()

    @pl.loop(0, NI // 32)
    def _(i):
        rows = pl.ds(pl.multiple_of(i * 32, 32), 32)
        out = permute_tiles([c_ref[rows, slot_cols(s)] for s in range(6)])
        for k in range(6):
            hi, lo = split(out[k])
            cph[rows, k * RUN:(k + 1) * RUN] = hi
            cpl[rows, k * RUN:(k + 1) * RUN] = lo

    out = permute_tiles([bm_ref[:, slot_cols(s)] for s in range(6)])
    for k in range(6):
        bmp[:, k * RUN:(k + 1) * RUN] = out[k]

    def permute_rows(slot, u, place):
        rows = pl.ds(pl.multiple_of(perm[slot] * RUN + u * SUB, SUB), SUB)
        target = pl.ds(pl.multiple_of(place, SUB), SUB)
        out = permute_tiles([b_ref[rows, slot_cols(s)] for s in range(6)])
        for k in range(6):
            bp[target, k * RUN:(k + 1) * RUN] = out[k]

    loads[1].wait()

    @pl.loop(0, 4)
    def _(u):
        for q in range(4):
            permute_rows(q, u, (u * 4 + q) * SUB)
        for q in range(2):
            permute_rows(4 + q, u, 512 + (u * 2 + q) * SUB)

    loads[2].wait()
    root = jnp.sqrt(im_ref[...])
    for i in range(4):
        rows = slice(i * 256, (i + 1) * 256)
        for j in range(i + 1):
            cols = slice(j * 256, (j + 1) * 256)
            block = f_ref[rows, cols]
            fh[rows, cols], fl[rows, cols] = split(block)
            fth[cols, rows], ftl[cols, rows] = split((block * root[:, cols]).T)
    for i in range(4):
        rows = slice(i * 256, (i + 1) * 256)
        depth = (i + 1) * 256
        for n in range(3):
            cols = slice(n * 256, (n + 1) * 256)
            w = dot3(fh[rows, :depth], fl[rows, :depth], cph[:depth, cols], cpl[:depth, cols])
            wh[rows, cols], wl[rows, cols] = split(w)
            wth[cols, rows], wtl[cols, rows] = split(w.T)
    for j in range(3):
        rows = slice(j * 256, (j + 1) * 256)
        for n in range(j, 3):
            cols = slice(n * 256, (n + 1) * 256)
            gram = dot3(wth[rows, :], wtl[rows, :], wh[:, cols], wl[:, cols])
            bp[rows, cols] = bp[rows, cols] - gram
    for i in range(4):
        rows = slice(i * 256, (i + 1) * 256)
        start = i * 256
        for n in range(3):
            cols = slice(n * 256, (n + 1) * 256)
            phi = dot3(fth[rows, start:], ftl[rows, start:], wh[start:, cols], wl[start:, cols])
            cph[rows, cols], cpl[rows, cols] = split(phi)
            wth[cols, rows], wtl[cols, rows] = split(phi.T)

    def put(rows, n, value):
        for half in range(2):
            tile = 2 * n + half
            part = value[:, half * RUN:(half + 1) * RUN]
            if tile < 4:
                oa_ref[tile, rows, :] = part
            else:
                for k in range(8):
                    start = (rows.start + k * SUB) // 2
                    for odd in range(2):
                        ol_ref[2 * (tile - 4) + odd, start:start + 16, :] = pack_half(
                            part[k * SUB:(k + 1) * SUB], odd
                        )

    for j in range(3):
        rows = slice(j * 256, (j + 1) * 256)
        for n in range(j, 3):
            cols = slice(n * 256, (n + 1) * 256)
            mass = dot3(wth[rows, :], wtl[rows, :], cph[:, cols], cpl[:, cols])
            if n == j:
                here = lax.broadcasted_iota(jnp.int32, (256, 256), 0)
                there = lax.broadcasted_iota(jnp.int32, (256, 256), 1)
                mass = mass + jnp.where(here == there, bmp[:, cols], 0.0)
            value = bp[rows, cols] - SHIFT * mass
            chi_ref[rows, cols], clo_ref[rows, cols] = split(mass)
            put(rows, n, value)
            if n != j:
                chi_ref[cols, rows], clo_ref[cols, rows] = split(mass.T)
                put(cols, j, value.T)


def condense(perm, factor, link, stiff, inner, outer):
    vmem = pl.BlockSpec(memory_space=pltpu.VMEM)
    shape = jax.ShapeDtypeStruct
    return pl.pallas_call(
        condense_kernel,
        out_shape=(
            shape((4, NB, RUN), F32),
            shape((4, NB // 2, RUN), F32),
            shape((NB, NB), BF16),
            shape((NB, NB), BF16),
        ),
        in_specs=[pl.BlockSpec(memory_space=pltpu.SMEM)] + [pl.BlockSpec(memory_space=pl.ANY)] * 3 + [vmem] * 2,
        out_specs=(vmem,) * 4,
        scratch_shapes=[
            pltpu.VMEM((NI, NB), BF16), pltpu.VMEM((NI, NB), BF16),
            pltpu.VMEM((NI, NI), BF16), pltpu.VMEM((NI, NI), BF16),
            pltpu.VMEM((NI, NI), BF16), pltpu.VMEM((NI, NI), BF16),
            pltpu.VMEM((NI, NB), BF16), pltpu.VMEM((NI, NB), BF16),
            pltpu.VMEM((NB, NI), BF16), pltpu.VMEM((NB, NI), BF16),
            pltpu.VMEM((NB, NB), F32), pltpu.VMEM((1, NB), F32),
            pltpu.VMEM((NI, NI), F32), pltpu.VMEM((NI, NB), F32), pltpu.VMEM((NB, NB), F32),
            pltpu.SemaphoreType.DMA((3,)),
        ],
        compiler_params=pltpu.CompilerParams(vmem_limit_bytes=VMEM_LIMIT),
        cost_estimate=pl.CostEstimate(flops=11 * 10**9, bytes_accessed=16 * 10**6, transcendentals=0),
        name="condense",
    )(perm, factor, link, stiff, inner, outer)


def modes_pack_kernel(runs, meta, q_ref, out_ref):
    light = meta[2]
    for c in range(COLS):
        for q in range(4):
            slot = jnp.where(light == 1, 4 + min(q, 1), q)
            block = runs[(meta[0] * COLS + c) * 6 + slot] // 2
            out_ref[c, q * SUB:(q + 1) * SUB, :] = q_ref[pl.ds(pl.multiple_of(block * SUB, SUB), SUB), :]


def modes_pack(runs, meta, modes):
    smem = pl.BlockSpec(memory_space=pltpu.SMEM)
    vmem = pl.BlockSpec(memory_space=pltpu.VMEM)
    return pl.pallas_call(
        modes_pack_kernel,
        out_shape=jax.ShapeDtypeStruct((COLS, RUN, MODES), F32),
        in_specs=[smem, smem, vmem],
        out_specs=vmem,
        compiler_params=pltpu.CompilerParams(vmem_limit_bytes=VMEM_LIMIT),
        name="modes_pack",
    )(runs, meta, modes)


def multiply_modes(parity, chi_ref, clo_ref, q_ref, out_ref, qh, ql):
    for u in range(4):
        block = q_ref[parity * 4 + u]
        rows = slice(u * RUN, (u + 1) * RUN)
        qh[rows, :], ql[rows, :] = split(block)
        block = q_ref[(1 - parity) * 4 + u, :64, :]
        rows = slice(512 + u * 64, 512 + (u + 1) * 64)
        qh[rows, :], ql[rows, :] = split(block)
    for j in range(3):
        rows = slice(j * 256, (j + 1) * 256)
        for n in range(2):
            cols = slice(n * 256, (n + 1) * 256)
            z = dot3(chi_ref[rows, :], clo_ref[rows, :], qh[:, cols], ql[:, cols])
            for half in range(2):
                for k in range(8):
                    start = (j * 256 + k * SUB) // 2
                    part = z[k * SUB:(k + 1) * SUB, half * RUN:(half + 1) * RUN]
                    for odd in range(2):
                        out_ref[n * 4 + half * 2 + odd, start:start + 16, :] = pack_half(part, odd)


def eye(n):
    return jnp.where(
        lax.broadcasted_iota(jnp.int32, (n, n), 0) == lax.broadcasted_iota(jnp.int32, (n, n), 1), 1.0, 0.0
    )


def exact(a, b, axis=1):
    return lax.dot_general(
        a, b, (((axis,), (0,)), ((), ())), precision=highest, preferred_element_type=F32
    )


STRIP = 16
STRIDE = 37


def invert_factor(m_ref, inv_ref, work, before_last):
    inv_ref[...] = jnp.zeros_like(inv_ref)
    lane = lax.broadcasted_iota(jnp.int32, (1, RUN), 1)
    height = lax.broadcasted_iota(jnp.int32, (STRIP, 1), 0)
    for k in range(4):
        if k == 3:
            before_last()
        block = slice(k * RUN, (k + 1) * RUN)
        work[:, :RUN] = m_ref[block, block]
        work[:, RUN:] = eye(RUN)

        @pl.loop(0, RUN // STRIP)
        def _(group):
            start = pl.multiple_of(group * STRIP, STRIP)
            strip = work[pl.ds(start, STRIP), :]
            square = strip[:, :RUN]
            columns = [
                jnp.sum(jnp.where(lane == start + j, square, 0.0), axis=1, keepdims=True)
                for j in range(STRIP)
            ]
            for j in range(STRIP):
                scale = lax.rsqrt(columns[j][j:j + 1])
                lead = strip[j:j + 1] * scale
                factor = jnp.where(height > j, columns[j] * scale, 0.0)
                strip = jnp.where(height == j, lead, strip - factor * lead)
                for k2 in range(j + 1, STRIP):
                    columns[k2] = columns[k2] - factor * (columns[k2][j:j + 1] * scale)
            later = jnp.where(lane >= start + STRIP, strip[:, :RUN], 0.0)
            work[...] = work[...] - exact(later, strip, 0)
            work[pl.ds(start, STRIP), :] = strip

        t = work[:, RUN:]
        left = None
        if k:
            left = exact(t, inv_ref[block, :k * RUN])
            inv_ref[block, :k * RUN] = left
        inv_ref[block, block] = t
        if k < 3:
            x = exact(t, m_ref[block, (k + 1) * RUN:])
            below = slice((k + 1) * RUN, 512)
            m_ref[below, below] = m_ref[below, below] - exact(x, x, 0)
            if k:
                inv_ref[below, :k * RUN] = inv_ref[below, :k * RUN] - exact(x, left, 0)
            inv_ref[below, block] = inv_ref[below, block] - exact(x, t, 0)


def exchange_kernel(
    heavy, oa, ol, chi, clo, sent, in_a, in_z,
    send_a, recv_a, send_z, recv_z, local_sem, oz, qh, ql, modes, send_q, recv_q, own_sem,
):
    row, col = lax.axis_index("row"), lax.axis_index("col")
    me = row * COLS + col
    barrier = pltpu.get_barrier_semaphore()

    @pl.loop(1, SUBS)
    def _(i):
        other = lax.rem(me + i, SUBS)
        pl.semaphore_signal(
            barrier, inc=1, device_id=(other // COLS, lax.rem(other, COLS)), device_id_type=MESH
        )

    pl.semaphore_wait(barrier, SUBS - 1)

    def place(target):
        target_row, target_col = target // COLS, lax.rem(target, COLS)
        rel = lax.rem(target_row // 4 + 4 - heavy, 4)
        light = lax.rem(target_col // 4 + heavy, 2)
        return target_row, target_col, rel, lax.rem(target_row, 4), light, lax.rem(target_col, 4)

    def first_row(rel, t):
        start = jnp.where(rel == 0, t * 128, jnp.where(rel == 2, t * 128 + 96, 512 + t * 64))
        return jnp.where(rel == 3, start + 32, start)

    def parts(target, use):
        target_row, target_col, rel, t, light, u = place(target)
        start = first_row(rel, t)
        for light_row in range(2):
            count = 32 if light_row else 96

            @pl.when((rel != 0) == (light_row == 1))
            def _():
                half = pl.multiple_of(start // 2, 16)
                use(
                    "z",
                    oz.at[target_col, pl.ds(half, count // 2)],
                    count // 2, target_row, target_col,
                )

                @pl.when(light == 0)
                def _():
                    use(
                        "a",
                        oa.at[u, pl.ds(pl.multiple_of(start, 32), count)],
                        count, target_row, target_col,
                    )

                @pl.when(light == 1)
                def _():
                    use(
                        "a",
                        ol.at[u, pl.ds(half, count // 2)],
                        count // 2, target_row, target_col,
                    )

    def box(kind, source, count):
        ref = in_a if kind == "a" else in_z
        return ref.at[pl.ds(pl.multiple_of(source * count, 16), count)]

    def remote(kind, source_ref, count, target_row, target_col):
        send, recv = (send_a, recv_a) if kind == "a" else (send_z, recv_z)
        return pltpu.make_async_remote_copy(
            src_ref=source_ref,
            dst_ref=box(kind, me, count),
            send_sem=send.at[target_row * COLS + target_col],
            recv_sem=recv.at[me],
            device_id=(target_row, target_col),
            device_id_type=MESH,
        )

    def keep(kind, source_ref, count, target_row, target_col):
        copy = pltpu.make_async_copy(source_ref, box(kind, me, count), local_sem)
        copy.start()
        copy.wait()

    def only(wanted, use):
        def chosen(kind, *a):
            if kind == wanted:
                use(kind, *a)
        return chosen

    def send_blocks(kind):
        @pl.loop(1, SUBS)
        def _(i):
            parts(lax.rem(me + i * STRIDE, SUBS), only(kind, lambda *a: remote(*a).start()))

    def modes_copy(light, c, source):
        rows = pl.ds(0, 64 if light else RUN)
        return pltpu.make_async_remote_copy(
            src_ref=sent.at[c, rows], dst_ref=modes.at[source, rows], send_sem=send_q.at[c],
            recv_sem=recv_q.at[source], device_id=(row, c), device_id_type=MESH,
        )

    def by_parity(c, use):
        for light in range(2):
            pl.when(lax.rem(c // 4 + heavy, 2) == light)(functools.partial(use, light))

    peers = [lax.rem(col + i, COLS) for i in (1, 7, 2, 6, 3, 5, 4)]
    for c in peers:
        by_parity(col, lambda light, c=c: modes_copy(light, c, col).start())
    own = pltpu.make_async_copy(sent.at[col], modes.at[col], own_sem)
    own.start()
    send_blocks("a")
    own.wait()
    for c in peers:
        by_parity(c, lambda light, c=c: modes_copy(light, c, c).wait_recv())
    multiply_modes(heavy % 2, chi, clo, modes, oz, qh, ql)
    send_blocks("z")
    parts(me, keep)

    def arrived(kind, source_ref, count, target_row, target_col):
        recv = recv_a if kind == "a" else recv_z

        @pl.loop(1, SUBS)
        def _(i):
            source = lax.rem(me + i, SUBS)
            here = box(kind, source, count)
            pltpu.make_async_copy(here, here, recv.at[source]).wait()

    parts(me, arrived)

    @pl.loop(1, SUBS)
    def _(i):
        target = lax.rem(me + i, SUBS)
        parts(target, lambda *a: remote(*a).wait_send())

    for c in peers:
        by_parity(col, lambda light, c=c: modes_copy(light, c, col).wait_send())


def exchange(heavy, oa, ol, chi, clo, sent):
    anywhere = pl.BlockSpec(memory_space=pl.ANY)
    vmem = pl.BlockSpec(memory_space=pltpu.VMEM)
    shape = jax.ShapeDtypeStruct
    return pl.pallas_call(
        functools.partial(exchange_kernel, heavy),
        out_shape=(shape((SUBS * 96, RUN), F32), shape((SUBS * 48, RUN), F32)),
        in_specs=[anywhere] * 2 + [vmem] * 2 + [anywhere],
        out_specs=(anywhere, anywhere),
        scratch_shapes=[pltpu.SemaphoreType.DMA((SUBS,))] * 4 + [
            pltpu.SemaphoreType.DMA,
            pltpu.VMEM((COLS, NB // 2, RUN), F32),
            pltpu.VMEM((NB, MODES), BF16),
            pltpu.VMEM((NB, MODES), BF16),
            pltpu.VMEM((COLS, RUN, MODES), F32),
            pltpu.SemaphoreType.DMA((COLS,)), pltpu.SemaphoreType.DMA((COLS,)),
            pltpu.SemaphoreType.DMA,
        ],
        compiler_params=pltpu.CompilerParams(
            collective_id=1 + heavy, has_side_effects=True, vmem_limit_bytes=VMEM_LIMIT
        ),
        name=f"exchange_{heavy}",
    )(oa, ol, chi, clo, sent)


def place_kernel(
    runs, meta, a_hbm, z_hbm, a_ref, z_ref, cols_ref, rows_ref, piece_ref, in_a, in_z, acc, zacc, ztall, sem
):
    rel, light = meta[1], meta[2]
    group = SUBS // 8

    def run(light_row, light_col):
        slots = [jnp.where(rel == 2, 3, jnp.where(rel == 1, 4, 5))] if light_row else [0, 1, 2]
        col_slots = [4, 5] if light_col else [0, 1, 2, 3]
        number = len(slots)
        height = 16 if light_col else SUB
        chunk = chunk_of_lane((height, RUN))

        def copies(g):
            a_rows = pl.ds(pl.multiple_of(g * group * number * height, 128), group * number * height)
            z_rows = pl.ds(pl.multiple_of(g * group * number * 16, 128), group * number * 16)
            return (
                pltpu.make_async_copy(a_hbm.at[a_rows], in_a.at[a_rows], sem.at[g, 0]),
                pltpu.make_async_copy(z_hbm.at[z_rows], in_z.at[z_rows], sem.at[g, 1]),
            )

        for g in range(8):
            for copy in copies(g):
                copy.start()
        acc[...] = jnp.zeros_like(acc)
        zacc[...] = jnp.zeros_like(zacc)

        def one(s):
            at = [runs[s * 6 + slot] // 4 for slot in slots]
            to = [runs[s * 6 + slot] // 2 for slot in col_slots]
            for p in range(number):
                zrows = pl.ds(pl.multiple_of(at[p] * 16, 16), 16)
                zacc[zrows, :] += in_z[pl.ds(pl.multiple_of((s * number + p) * 16, 16), 16), :]
            for p in range(number):
                piece = in_a[pl.ds(pl.multiple_of((s * number + p) * height, height), height), :]
                new = []
                for q in range(len(to)):
                    tile, place = to[q] // 4, lax.rem(to[q], 4)
                    for half in range(SUB // height):
                        rows = pl.ds(pl.multiple_of(at[p] * SUB + half * height, height), height)
                        moved = pltpu.roll(piece, lax.rem(place + 8 - q - 2 * half, 4) * SUB, 1)
                        moved = jnp.where(chunk == place, moved, 0.0)
                        new.append((q, tile, rows, acc[q, tile, rows, :] + moved))
                for q, tile, rows, value in new:
                    acc[q, tile, rows, :] = value

        @pl.loop(0, 8)
        def _(g):
            for copy in copies(g):
                copy.wait()

            @pl.loop(0, group, unroll=4)
            def _(i):
                one(g * group + i)

    for light_row in range(2):
        for light_col in range(2):
            pl.when(((rel != 0) == (light_row == 1)) & (light == light_col))(
                functools.partial(run, light_row, light_col)
            )
    for k in range(8):
        a_ref[:, k * RUN:(k + 1) * RUN] = (acc[0, k] + acc[1, k]) + (acc[2, k] + acc[3, k])
    for k in range(16):
        piece = zacc[k * 16:(k + 1) * 16, :]
        ztall[k * SUB:k * SUB + 16, :] = piece
        ztall[k * SUB + 16:(k + 1) * SUB, :] = pltpu.roll(piece, 64, 1)
    z_ref[...] = ztall[...].T[:64, :]
    cols_ref[...] = a_ref[:, :RUN].T[:64, :]
    piece_ref[...] = cols_ref[:, :RUN]
    rows_ref[:, :1024] = a_ref[:SUB, :]
    rows_ref[:, 1024:] = ztall[:SUB, :]


def place(runs, meta, in_a, in_z):
    smem = pl.BlockSpec(memory_space=pltpu.SMEM)
    vmem = pl.BlockSpec(memory_space=pltpu.VMEM)
    shape = jax.ShapeDtypeStruct
    return pl.pallas_call(
        place_kernel,
        out_shape=(
            shape((512, 1024), F32), shape((64, 512), F32), shape((64, 512), F32), shape((SUB, 1152), F32),
            shape((64, RUN), F32),
        ),
        in_specs=[smem, smem] + [pl.BlockSpec(memory_space=pl.ANY)] * 2,
        out_specs=(vmem,) * 5,
        scratch_shapes=[
            pltpu.VMEM((SUBS * 96, RUN), F32),
            pltpu.VMEM((SUBS * 48, RUN), F32),
            pltpu.VMEM((4, 8, 512, RUN), F32),
            pltpu.VMEM((256, RUN), F32),
            pltpu.VMEM((512, RUN), F32),
            pltpu.SemaphoreType.DMA((8, 2)),
        ],
        compiler_params=pltpu.CompilerParams(vmem_limit_bytes=VMEM_LIMIT),
        name="place",
    )(runs, meta, in_a, in_z)


def panel_kernel(
    a_hbm, z_hbm, cols_ref, rows_ref, piece_ref, out_ref, zout_ref,
    a_ref, z_ref, col_box, row_box, ih, il, lth, ltl, uh, ul, inv_ref, m_ref, work, strips, mine,
    send_c, recv_c, send_r, recv_r, send_f, local_sem, send_p, recv_p, send_m, recv_m, send_n,
):
    row, col = lax.axis_index("row"), lax.axis_index("col")
    barrier = pltpu.get_barrier_semaphore()
    peers_c = [lax.rem(col + i, COLS) for i in (1, 7, 2, 6, 3, 5, 4)]
    peers_r = [lax.rem(row + 2 * i, ROWS) for i in (1, 7, 2, 6, 3, 5, 4)]
    partner = row + 1 - 2 * lax.rem(row, 2)
    for c in peers_c:
        pl.semaphore_signal(barrier, inc=1, device_id=(row, c), device_id_type=MESH)
    for r in peers_r + [partner]:
        pl.semaphore_signal(barrier, inc=1, device_id=(r, col), device_id_type=MESH)
    pl.semaphore_wait(barrier, 15)

    def col_place(c):
        return pl.ds(pl.multiple_of(c * 64, 64), 64)

    def row_place(r):
        return pl.ds(pl.multiple_of(lax.rem(r, 8) * 64 + r // 8 * SUB, SUB), SUB)

    sends = [
        pltpu.make_async_remote_copy(
            src_ref=piece_ref, dst_ref=strips.at[col_place(col)], send_sem=send_p.at[c],
            recv_sem=recv_p.at[col], device_id=(row, c), device_id_type=MESH,
        )
        for c in peers_c
    ]
    for send in sends:
        send.start()
    locals_ = [
        pltpu.make_async_copy(cols_ref, col_box.at[col_place(col)], local_sem.at[0]),
        pltpu.make_async_copy(rows_ref, row_box.at[row_place(row)], local_sem.at[1]),
        pltpu.make_async_copy(a_hbm, a_ref, local_sem.at[2]),
        pltpu.make_async_copy(z_hbm, z_ref, local_sem.at[3]),
    ]
    for copy in locals_:
        copy.start()
    strips[col_place(col), :] = piece_ref[...]
    for c in peers_c:
        here = strips.at[col_place(c)]
        pltpu.make_async_copy(here, here, recv_p.at[c]).wait()
    mine[...] = strips[...].T[:SUB, :]

    def gather_rows(source_ref, box, send, recv, again):
        def copy(ref, r, sem, origin):
            return pltpu.make_async_remote_copy(
                src_ref=ref, dst_ref=box.at[row_place(origin)], send_sem=sem.at[r],
                recv_sem=recv.at[origin], device_id=(r, col), device_id_type=MESH,
            )

        first = [copy(source_ref, r, send, row) for r in peers_r + [partner]]
        handed = []

        def forward():
            for r in peers_r:
                here = box.at[row_place(r)]
                pltpu.make_async_copy(here, here, recv.at[r]).wait()
                onward = pltpu.make_async_remote_copy(
                    src_ref=here, dst_ref=here, send_sem=again.at[r],
                    recv_sem=recv.at[r], device_id=(partner, col), device_id_type=MESH,
                )
                onward.start()
                handed.append(onward)

        def finish():
            for r in [partner] + [lax.rem(partner + 2 * i, ROWS) for i in (1, 7, 2, 6, 3, 5, 4)]:
                here = box.at[row_place(r)]
                pltpu.make_async_copy(here, here, recv.at[r]).wait()

        def drained():
            for onward in handed:
                onward.wait_send()

        for send_one in first:
            send_one.start()
        sends.extend(first)
        return forward, finish, drained

    forward, finish, drained = gather_rows(mine, m_ref, send_m, recv_m, send_n)
    m_ref[row_place(row), :] = mine[...]
    forward()
    col_sends = [
        pltpu.make_async_remote_copy(
            src_ref=cols_ref, dst_ref=col_box.at[col_place(col)], send_sem=send_c.at[c],
            recv_sem=recv_c.at[col], device_id=(row, c), device_id_type=MESH,
        )
        for c in peers_c
    ]
    forward_rows, finish_rows, drained_rows = gather_rows(rows_ref, row_box, send_r, recv_r, send_f)
    for send in col_sends:
        send.start()
    sends.extend(col_sends)
    finish()
    drained()
    invert_factor(m_ref, inv_ref, work, forward_rows)
    ih[...], il[...] = split(inv_ref[...])
    for copy in locals_:
        copy.wait()
    for c in peers_c:
        here = col_box.at[col_place(c)]
        pltpu.make_async_copy(here, here, recv_c.at[c]).wait()
    bh, bl = split(col_box[...])
    for i in range(2):
        rows = slice(i * 256, (i + 1) * 256)
        lth[:, rows], ltl[:, rows] = split(dot3(ih[rows, :], il[rows, :], bh, bl).T)
    finish_rows()
    for n in range(3):
        cols = slice(n * 384, (n + 1) * 384)
        bh, bl = split(row_box[:, cols])
        uh[:, cols], ul[:, cols] = split(dot3(ih[...], il[...], bh, bl))
    for i in range(2):
        rows = slice(i * 256, (i + 1) * 256)
        for n in range(4):
            cols = slice(n * 256, (n + 1) * 256)
            out_ref[rows, cols] = a_ref[rows, cols] - dot3(lth[rows, :], ltl[rows, :], uh[:, cols], ul[:, cols])
        last = dot3(lth[rows, :], ltl[rows, :], uh[:, 1024:], ul[:, 1024:])
        zout_ref[:, rows] = z_ref[:, rows] - last.T[:64, :]
    drained_rows()
    for send in sends:
        send.wait_send()


def panel(shifted, modes_local, cols, rows, piece):
    vmem = pl.BlockSpec(memory_space=pltpu.VMEM)
    anywhere = pl.BlockSpec(memory_space=pl.ANY)
    shape = jax.ShapeDtypeStruct
    return pl.pallas_call(
        panel_kernel,
        out_shape=(shape((512, 1024), F32), shape((64, 512), F32)),
        in_specs=[anywhere] * 4 + [vmem],
        out_specs=(vmem, vmem),
        scratch_shapes=[
            pltpu.VMEM((512, 1024), F32), pltpu.VMEM((64, 512), F32),
            pltpu.VMEM((512, 512), F32), pltpu.VMEM((512, 1152), F32),
            pltpu.VMEM((512, 512), BF16), pltpu.VMEM((512, 512), BF16),
            pltpu.VMEM((512, 512), BF16), pltpu.VMEM((512, 512), BF16),
            pltpu.VMEM((512, 1152), BF16), pltpu.VMEM((512, 1152), BF16),
            pltpu.VMEM((PANEL, PANEL), F32), pltpu.VMEM((PANEL, PANEL), F32),
            pltpu.VMEM((RUN, 2 * RUN), F32), pltpu.VMEM((PANEL, RUN), F32), pltpu.VMEM((SUB, PANEL), F32),
            pltpu.SemaphoreType.DMA((COLS,)), pltpu.SemaphoreType.DMA((COLS,)),
            pltpu.SemaphoreType.DMA((ROWS,)), pltpu.SemaphoreType.DMA((ROWS,)),
            pltpu.SemaphoreType.DMA((ROWS,)), pltpu.SemaphoreType.DMA((4,)),
            pltpu.SemaphoreType.DMA((COLS,)), pltpu.SemaphoreType.DMA((COLS,)),
            pltpu.SemaphoreType.DMA((ROWS,)), pltpu.SemaphoreType.DMA((ROWS,)),
            pltpu.SemaphoreType.DMA((ROWS,)),
        ],
        compiler_params=pltpu.CompilerParams(
            collective_id=5, has_side_effects=True, vmem_limit_bytes=VMEM_LIMIT
        ),
        name="panel",
    )(shifted, modes_local, cols, rows, piece)


def slot_order(interface_ids):
    runs = interface_ids[:, ::RUN] // RUN
    kinds = runs % 4
    first = kinds[0]
    heavy = jnp.argmax(jnp.sum(first[None, :] == jnp.arange(4)[:, None], axis=1)).astype(jnp.int32)
    rel = (kinds - heavy) % 4
    key = jnp.where(rel == 1, 2, jnp.where(rel == 2, 1, rel)) * 8 + jnp.arange(6)
    slot = jnp.sum(key[:, None, :] < key[:, :, None], axis=2)
    hit = slot[:, :, None] == jnp.arange(6)
    ordered = jnp.sum(jnp.where(hit, runs[:, :, None], 0), axis=1)
    origin = jnp.sum(jnp.where(hit, jnp.arange(6)[None, :, None], 0), axis=1)
    return heavy, ordered.astype(jnp.int32), origin.astype(jnp.int32)


def body(
    inverse_factor,
    coupling,
    boundary_stiffness,
    interior_mass,
    boundary_mass,
    interface_ids,
    trial_modes,
):
    row, col = lax.axis_index("row"), lax.axis_index("col")
    heavy, ordered, origin = slot_order(interface_ids)
    me = row * COLS + col
    perm = lax.dynamic_index_in_dim(origin, me, 0, keepdims=False)
    runs = ordered.reshape(-1)
    meta = jnp.stack([row, (row // 4 + 4 - heavy) % 4, (col // 4 + heavy) % 2]).astype(jnp.int32)
    sent = modes_pack(runs, meta, trial_modes)
    oa, ol, chi, clo = condense(
        perm, inverse_factor[0], coupling[0], boundary_stiffness[0], interior_mass, boundary_mass
    )
    in_a, in_z = lax.switch(
        heavy, [functools.partial(exchange, h) for h in range(4)], oa, ol, chi, clo, sent
    )
    shifted, modes_local, cols, rows, piece = place(runs, meta, in_a, in_z)
    return panel(shifted, modes_local, cols, rows, piece)


def solution(mesh):
    return jax.shard_map(
        body,
        mesh=mesh,
        in_specs=(
            P(("row", "col"), None, None),
            P(("row", "col"), None, None),
            P(("row", "col"), None, None),
            P(("row", "col"), None),
            P(("row", "col"), None),
            P(),
            P("col", None),
        ),
        out_specs=(P("row", "col"), P("col", "row")),
        check_vma=False,
    )
```
